256 devices in a mesh: bra: 8 (over z), ket: 8 (over y, core), pair: 4 (over x).
Axes of the slice: x: 4, y: 4, z: 8, core: 2. Of those that a mesh axis runs over, the one named last changes fastest.
Arguments:
- amplitudes: bfloat16 [1536, 64, 1536], P('pair', ('bra', 'ket')), may hold values from -6 to 6
- integrals: bfloat16 [64, 32, 128, 1536], P(('bra', 'ket'), 'pair'), may hold values from -0.09375 to 0.09375
- screen_list: int32 [64, 32], P(('bra', 'ket')), may hold values from 0 to 11
- block_owner: int32 [64, 32], P(('bra', 'ket')), may hold values from 0 to 63, all different within a row
- mirror_map: int32 [64, 1536], replicated, may hold values from 0 to 1535, as said below
- pair_virt: int32 [64, 2, 1536], P(('bra', 'ket')), may hold values from 0 to 2047, as said below
- vir_energy: float32 [2048], replicated, may hold values from 0.1 to 1.5
- pair_energy: float32 [1536], P('pair'), may hold values from -1.5 to -0.4
Outputs:
- new_amplitudes: bfloat16 [1536, 64, 1536], P('pair', ('bra', 'ket'))
The draws below stay inside these ranges and needn't reach their ends.
Inputs may be any that keep to these rules, and one draw needn't show every extreme that they name: `block_owner`: the 32 entries of a row are distinct. `mirror_map`: every row is a permutation of 0 to 1535, and row t + 32 is the inverse permutation of row t. `pair_virt`: if position p of tile t < 32 holds the orbitals (a, b), position mirror_map[t, p] of tile t + 32 holds (b, a).
All inputs are finite; a program needn't handle non-finite values.
Results may differ from the reference program's by a relative error of at most 0.0045.
Values may be sent and summed in bfloat16 or wider, within the bound.
No kernel may reach another device: no remote copies, remote signals or barrier semaphores. Data moves between devices by JAX's collectives and lax.ppermute only.
A program may use at most 64 MiB of HBM per device.

```python
import math
import jax
import jax.numpy as jnp
from jax import lax

NV = 2048
BLK = 1536
SEG = 128
OCC = 1536
TILES = 64
NBLK = 32
SEGS = 12


def mirror_helper(key):
    half_tiles = TILES // 2
    keys = jax.random.split(jax.random.fold_in(key, 7), half_tiles)
    forward = jax.vmap(lambda single: jax.random.permutation(single, BLK))(keys).astype(jnp.int32)

    def invert(perm):
        return jnp.zeros((BLK,), jnp.int32).at[perm].set(jnp.arange(BLK, dtype=jnp.int32))
    inverse = jax.vmap(invert)(forward)
    return (forward, inverse)


def draw_mirror_map(key, part):
    forward, inverse = mirror_helper(key)
    return jnp.concatenate([forward, inverse], 0)


def draw_pair_virt(key, part):
    half_tiles = TILES // 2
    forward, inverse = mirror_helper(key)
    first = jax.random.randint(jax.random.fold_in(key, 11), (half_tiles, BLK), 0, NV).astype(jnp.int32)
    second = jax.random.randint(jax.random.fold_in(key, 13), (half_tiles, BLK), 0, NV).astype(jnp.int32)
    first = first.at[0, 0].set(0).at[0, 1].set(NV - 1)
    lower_pairs = jnp.stack([first, second], 1)
    upper_first = jnp.take_along_axis(second, inverse, axis=1)
    upper_second = jnp.take_along_axis(first, inverse, axis=1)
    upper_pairs = jnp.stack([upper_first, upper_second], 1)
    return jnp.concatenate([lower_pairs, upper_pairs], 0)


def place_ends(entries, key, smallest, largest):
    place = [jax.random.randint(jax.random.fold_in(key, axis), (), 0, length) for axis, length in enumerate(entries.shape)]
    longest = entries.shape.index(max(entries.shape))
    neighbour = place[:longest] + [(place[longest] + 1) % entries.shape[longest]] + place[longest + 1:]
    return entries.at[tuple(place)].set(smallest).at[tuple(neighbour)].set(largest)


def shard_levels(own_key, shape, cuts, smallest, top_value):
    gain, own = 1.0, jax.random.fold_in(own_key, 6)
    for axis_at, shards_of in cuts:
        steps = jnp.exp(jax.random.uniform(jax.random.fold_in(own, axis_at), (shards_of,), jnp.float32, smallest / len(cuts), top_value / len(cuts)))
        gain = gain * jnp.repeat(steps, shape[axis_at] // shards_of).reshape([-1 if axis == axis_at else 1 for axis in range(len(shape))])
    return gain


def distinct(own_key, rows, number_of, top, lift):
    order = jax.random.permutation(jax.random.fold_in(own_key, 1), number_of)
    boost = order
    for power in range(3):
        boost = boost * boost // number_of
    boost = boost * lift // number_of
    tickets = jax.random.randint(jax.random.fold_in(own_key, 2), (rows, number_of), 0, 4096) + boost
    holders = jax.random.permutation(jax.random.fold_in(own_key, 3), rows)[jnp.arange(number_of) % rows]
    tickets = jnp.where(jnp.arange(rows)[:, None] == holders[None, :], 1 << 14, tickets)
    score = tickets * number_of + jnp.arange(number_of)
    return lax.top_k(score.astype(jnp.int32), top)[1].astype(jnp.int32)


def normal_values(rng, dims, deviation, limit, cuts=(), kind=jnp.bfloat16):
    result = deviation * jax.random.normal(rng, dims, jnp.float32)
    if cuts:
        result = result * shard_levels(rng, dims, cuts, -0.22, 0.18)
    return jnp.clip(result, -limit, limit).astype(kind)


def setup_inputs(seed: int = 0) -> dict:
    key_list = jax.random.split(jax.random.key(seed), 9)
    amplitudes = normal_values(key_list[0], (OCC, TILES, BLK), 1.0, 6.0, ((0, 4), (1, 64)))
    integrals = normal_values(key_list[1], (TILES, NBLK, SEG, BLK), (NBLK * SEG) ** -0.5, 0.09375, ((0, 64), (1, 4)))
    screen_list = place_ends(jax.random.randint(key_list[2], (TILES, NBLK), 0, SEGS), jax.random.fold_in(key_list[2], 1), 0, SEGS - 1).astype(jnp.int32)
    block_owner = distinct(key_list[3], TILES, TILES, NBLK, 8192)
    mirror_map = draw_mirror_map(jax.random.fold_in(key_list[8], 71), 0)
    pair_virt = draw_pair_virt(jax.random.fold_in(key_list[8], 71), 0)
    vir_energy = jnp.clip(jnp.exp(jax.random.uniform(key_list[6], (NV,), jnp.float32, math.log(0.1), math.log(1.5))), 0.1, 1.5)
    pair_energy = jnp.clip(-1.5 + 1.1 * jax.random.uniform(key_list[7], (OCC,), jnp.float32) ** shard_levels(key_list[7], (OCC,), ((0, 4),), -0.2, 0.2), -1.5, -0.4)
    return {"amplitudes": amplitudes, "integrals": integrals, "screen_list": screen_list, "block_owner": block_owner, "mirror_map": mirror_map, "pair_virt": pair_virt, "vir_energy": vir_energy, "pair_energy": pair_energy}


def permute_columns(tile_data, indices):
    return jnp.take(tile_data, indices, axis=1)


def reference(amplitudes, integrals, screen_list, block_owner, mirror_map, pair_virt, vir_energy, pair_energy):
    occupied, tile_count, block_len = amplitudes.shape
    half_tiles = tile_count // 2
    seg_width = integrals.shape[2]
    seg_count = block_len // seg_width
    permute_tiles = jax.vmap(permute_columns, in_axes=(1, 0), out_axes=1)
    permute_rows = jax.vmap(permute_columns, in_axes=(0, 0), out_axes=0)
    lower_raw = amplitudes[:, :half_tiles, :]
    upper_raw = amplitudes[:, half_tiles:, :]
    map_lower = mirror_map[:half_tiles]
    map_upper = mirror_map[half_tiles:]
    sym_fold = ((lower_raw.astype(jnp.float32) + permute_tiles(upper_raw, map_lower).astype(jnp.float32)) * 0.5).astype(jnp.bfloat16)
    anti_fold = ((upper_raw.astype(jnp.float32) - permute_tiles(lower_raw, map_upper).astype(jnp.float32)) * 0.5).astype(jnp.bfloat16)
    sym_segments = sym_fold.reshape(occupied, half_tiles, seg_count, seg_width)
    anti_segments = anti_fold.reshape(occupied, half_tiles, seg_count, seg_width)

    def one_tile(packed):
        tile_id, owners_row, segments_row, blocks = packed
        source = owners_row % half_tiles
        from_sym = sym_segments[:, source, segments_row, :]
        from_anti = anti_segments[:, source, segments_row, :]
        operand = jnp.where(tile_id >= half_tiles, from_anti, from_sym)
        return jnp.dot(operand.reshape(occupied, -1), blocks.reshape(-1, block_len), preferred_element_type=jnp.float32)

    ladder = lax.map(one_tile, (jnp.arange(tile_count, dtype=jnp.int32), block_owner, screen_list, integrals))
    resid_lower = ladder[:half_tiles] - permute_rows(ladder[half_tiles:], map_lower)
    resid_upper = ladder[half_tiles:] + permute_rows(ladder[:half_tiles], map_upper)
    residual = jnp.transpose(jnp.concatenate([resid_lower, resid_upper], 0), (1, 0, 2))
    energy_first = jnp.take(vir_energy, pair_virt[:, 0, :])
    energy_second = jnp.take(vir_energy, pair_virt[:, 1, :])
    denominator = pair_energy[:, None, None] - energy_first[None] - energy_second[None]
    return (amplitudes.astype(jnp.float32) + residual / denominator).astype(jnp.bfloat16)
```

```python
import functools

import jax
import jax.numpy as jnp
from jax import lax
from jax.experimental import pallas as pl
from jax.experimental.pallas import tpu as pltpu
from jax.sharding import PartitionSpec as P

COLS = 256
VMEM = 48 * 1024 * 1024


def one_hot(row, length, width):
    number = lax.broadcasted_iota(jnp.int32, (length, width), 0)
    return jnp.where(number == row, 1.0, 0.0).astype(jnp.bfloat16)


def fold_body(shifts, facts, maps, *refs):
    count = len(shifts)
    tiles, out = refs[: 2 * count], refs[2 * count]
    base, other, folded, base_sem, other_sem, out_sem = refs[2 * count + 1 :]
    z = facts[0]
    sign = jnp.where(z < 4, 1.0, -1.0).astype(jnp.float32)
    rows, length = folded.shape[1:]

    def fetch(i, turned):
        first, second = tiles[2 * i], tiles[2 * i + 1]
        if turned:
            first, second = second, first
        return (
            pltpu.make_async_copy(first, base.at[i], base_sem.at[i]),
            pltpu.make_async_copy(second, other.at[i], other_sem.at[i]),
        )

    def straight(shift):
        moved = z + shift
        return ((moved + 8) & 7) >> 2 == z >> 2

    for i, shift in enumerate(shifts):
        for turned in (False, True):

            @pl.when(straight(shift) != turned)
            def _():
                for copy in fetch(i, turned):
                    copy.start()

    for i, shift in enumerate(shifts):
        low = (z + shift + 8) & 3
        for copy in fetch(i, False):
            copy.wait()

        def column(c, carry):
            start = pl.multiple_of(c * COLS, COLS)
            picks = one_hot(maps[low, :, pl.ds(start, COLS)], length, COLS)
            turned = jnp.dot(other[i], picks, preferred_element_type=jnp.float32)
            mine = base[i, :, pl.ds(start, COLS)].astype(jnp.float32)
            folded[i, :, pl.ds(start, COLS)] = ((mine + sign * turned) * 0.5).astype(jnp.bfloat16)
            return carry

        lax.fori_loop(0, length // COLS, column, 0)

        for receiver in range(8):
            for half in range(2):
                segment = facts[1 + receiver * 8 + low + 4 * half]

                @pl.when(segment >= 0)
                def _():
                    start = pl.multiple_of(segment * 128, 128)
                    pltpu.make_async_copy(
                        folded.at[i, :, pl.ds(start, 128)],
                        out.at[receiver, 2 * i + half],
                        out_sem.at[i, receiver, half],
                    ).start()

    for i, shift in enumerate(shifts):
        low = (z + shift + 8) & 3
        for receiver in range(8):
            for half in range(2):

                @pl.when(facts[1 + receiver * 8 + low + 4 * half] >= 0)
                def _():
                    pltpu.make_async_copy(
                        folded.at[i, :, pl.ds(0, 128)],
                        out.at[receiver, 2 * i + half],
                        out_sem.at[i, receiver, half],
                    ).wait()


def fold(shifts, facts, maps, tiles):
    rows, length = tiles[0].shape
    count = len(shifts)
    whole = pltpu.VMEM((count, rows, length), jnp.bfloat16)
    return pl.pallas_call(
        functools.partial(fold_body, shifts),
        in_specs=[pl.BlockSpec(memory_space=pltpu.SMEM), pl.BlockSpec(memory_space=pltpu.VMEM)]
        + [pl.BlockSpec(memory_space=pl.ANY)] * (2 * count),
        out_specs=pl.BlockSpec(memory_space=pl.ANY),
        out_shape=jax.ShapeDtypeStruct((8, 2 * count, rows, 128), jnp.bfloat16),
        scratch_shapes=[
            whole,
            whole,
            whole,
            pltpu.SemaphoreType.DMA((count,)),
            pltpu.SemaphoreType.DMA((count,)),
            pltpu.SemaphoreType.DMA((count, 8, 2)),
        ],
        compiler_params=pltpu.CompilerParams(vmem_limit_bytes=VMEM),
        cost_estimate=pl.CostEstimate(
            flops=2 * count * rows * length * length,
            bytes_accessed=count * rows * (4 * length + 16 * 256),
            transcendentals=0,
        ),
        name="fold",
    )(facts, maps, *tiles)


def ladder_body(facts, send_map, blocks, near, odd, opposite, ladder, sent, operand, rounded, sem):
    step = pl.program_id(0)
    slots = operand.shape[1] // 128
    length = rounded.shape[1]

    @pl.when(step == 0)
    def _():
        def place(k):
            return operand.at[:, pl.ds(k * 128, 128)]

        for k in range(slots):
            tile = facts[1 + k]
            z, ket = tile >> 3, tile & 7
            away, half = (z - facts[0] + 8) & 3, z >> 2

            @pl.when(away == 0)
            def _():
                pltpu.make_async_copy(near.at[ket, half], place(k), sem.at[k]).start()

            @pl.when((away & 1) == 1)
            def _():
                source = odd.at[ket, (away >> 1) * 2 + half]
                pltpu.make_async_copy(source, place(k), sem.at[k]).start()

            @pl.when(away == 2)
            def _():
                pltpu.make_async_copy(opposite.at[ket, half], place(k), sem.at[k]).start()

        for k in range(slots):
            pltpu.make_async_copy(near.at[0, 0], place(k), sem.at[k]).wait()

    total = jnp.dot(operand[...], blocks[...], preferred_element_type=jnp.float32)
    ladder[...] = total
    rounded[:, pl.ds(pl.multiple_of(step * COLS, COLS), COLS)] = total.astype(jnp.bfloat16)

    @pl.when(step == pl.num_programs(0) - 1)
    def _():
        def column(c, carry):
            start = pl.multiple_of(c * COLS, COLS)
            picks = one_hot(send_map[:, pl.ds(start, COLS)], length, COLS)
            moved = jnp.dot(rounded[...], picks, preferred_element_type=jnp.float32)
            sent[:, pl.ds(start, COLS)] = moved.astype(jnp.bfloat16)
            return carry

        lax.fori_loop(0, length // COLS, column, 0)


def ladder_of(facts, send_map, blocks, near, odd, opposite):
    depth, length = blocks.shape
    rows = near.shape[2]
    held = pl.BlockSpec(memory_space=pl.ANY)
    return pl.pallas_call(
        ladder_body,
        grid=(length // COLS,),
        in_specs=[
            pl.BlockSpec(memory_space=pltpu.SMEM),
            pl.BlockSpec((1, length), lambda n: (0, 0)),
            pl.BlockSpec((depth, COLS), lambda n: (0, n)),
            held,
            held,
            held,
        ],
        out_specs=[
            pl.BlockSpec((rows, COLS), lambda n: (0, n)),
            pl.BlockSpec((rows, length), lambda n: (0, 0)),
        ],
        out_shape=[
            jax.ShapeDtypeStruct((rows, length), jnp.float32),
            jax.ShapeDtypeStruct((rows, length), jnp.bfloat16),
        ],
        scratch_shapes=[
            pltpu.VMEM((rows, depth), jnp.bfloat16),
            pltpu.VMEM((rows, length), jnp.bfloat16),
            pltpu.SemaphoreType.DMA((depth // 128,)),
        ],
        compiler_params=pltpu.CompilerParams(
            vmem_limit_bytes=VMEM, dimension_semantics=("arbitrary",)
        ),
        cost_estimate=pl.CostEstimate(
            flops=2 * rows * depth * length,
            bytes_accessed=2 * depth * (rows + length),
            transcendentals=0,
        ),
        name="ladder",
    )(facts, send_map, blocks, near, odd, opposite)


def shifted(block, by):
    return lax.ppermute(block, "bra", [(i, (i + by) % 8) for i in range(8)])


def energies(table, indices):
    number = lax.broadcasted_iota(jnp.int32, (table.shape[0], 1), 0)
    return jnp.sum(jnp.where(number == indices[None, :], table[:, None], 0.0), axis=0)


def local(
    amplitudes, integrals, screen_list, block_owner, mirror_map, pair_virt, vir_energy, pair_energy
):
    z, ket = lax.axis_index("bra"), lax.axis_index("ket")
    own = amplitudes[:, 0, :]
    rows, length = own.shape
    all_blocks = lax.all_gather(integrals[0], "pair", axis=0, tiled=True).reshape(-1, length)

    wanted = lax.all_gather(block_owner[0] * 16 + screen_list[0], "ket", axis=0)
    served = jnp.arange(8, dtype=jnp.int32) * 8 + ket
    match = (wanted >> 4)[:, None, :] == served[None, :, None]
    asked = jnp.max(jnp.where(match, wanted[:, None, :] & 15, -1), axis=2)
    fold_facts = jnp.concatenate([z.astype(jnp.int32)[None], asked.reshape(-1)])
    ladder_facts = jnp.concatenate([z.astype(jnp.int32)[None], block_owner[0]])
    grid_maps = mirror_map.reshape(2, 4, 8, length)
    half_maps = lax.dynamic_index_in_dim(grid_maps, z >> 2, 0, keepdims=False)
    maps = lax.dynamic_index_in_dim(half_maps, ket, 1, keepdims=True)
    send_map = lax.dynamic_index_in_dim(mirror_map, ((z + 4) & 7) * 8 + ket, 0, keepdims=True)

    up1, down1 = shifted(own, -1), shifted(own, 1)
    up2, down2 = shifted(up1, -1), shifted(down1, 1)
    up3, down3 = shifted(up2, -1), shifted(down2, 1)
    cut = rows // 2
    far = jnp.concatenate([shifted(up3[:cut], -1), shifted(down3[cut:], 1)], axis=0)

    def exchange(block):
        return lax.all_to_all(block, "ket", split_axis=0, concat_axis=0, tiled=True)

    opposite = exchange(fold((2,), fold_facts, maps, (up2, down2)))
    odd = exchange(fold((1, 3), fold_facts, maps, (up1, down3, up3, down1)))
    near = exchange(fold((0,), fold_facts, maps, (own, far)))
    ladder, sent = ladder_of(ladder_facts, send_map, all_blocks, near, odd, opposite)
    partner = shifted(sent, 4)
    direction = jnp.where(z >= 4, 1.0, -1.0).astype(jnp.float32)
    residual = ladder + direction * partner.astype(jnp.float32)
    first = energies(vir_energy, pair_virt[0, 0])
    second = energies(vir_energy, pair_virt[0, 1])
    denominator = pair_energy[:, None] - first[None, :] - second[None, :]
    updated = own.astype(jnp.float32) + residual / denominator
    return updated.astype(jnp.bfloat16)[:, None, :]


def solution(mesh):
    placed = (
        P("pair", ("bra", "ket"), None),
        P(("bra", "ket"), "pair", None, None),
        P(("bra", "ket"), None),
        P(("bra", "ket"), None),
        P(),
        P(("bra", "ket"), None, None),
        P(),
        P("pair"),
    )
    return jax.shard_map(
        local,
        mesh=mesh,
        in_specs=placed,
        out_specs=P("pair", ("bra", "ket"), None),
        check_vma=False,
    )
```

```python
import functools

import jax
import jax.numpy as jnp
from jax import lax
from jax.experimental import pallas as pl
from jax.experimental.pallas import tpu as pltpu
from jax.sharding import PartitionSpec as P

COLS = 256
VMEM = 40 * 1024 * 1024


def one_hot(row, length, width):
    number = lax.broadcasted_iota(jnp.int32, (length, width), 0)
    return jnp.where(number == row, 1.0, 0.0).astype(jnp.bfloat16)


def fold_body(shifts, facts, maps, *refs):
    count = len(shifts)
    tiles = refs[: 3 if shifts == (0,) else 2 * count]
    out, base, other, folded, base_sem, other_sem, out_sem = refs[-7:]
    z = facts[0]
    sign = jnp.where(z < 4, 1.0, -1.0).astype(jnp.float32)
    rows, length = folded.shape[1:]

    def fetch(i, turned):
        if shifts[i] == 0:
            cut = tiles[1].shape[0]
            return (
                pltpu.make_async_copy(tiles[0], base.at[i], base_sem.at[i]),
                pltpu.make_async_copy(tiles[1], other.at[i, pl.ds(0, cut)], other_sem.at[i, 0]),
                pltpu.make_async_copy(tiles[2], other.at[i, pl.ds(cut, cut)], other_sem.at[i, 1]),
            )
        first, second = tiles[2 * i], tiles[2 * i + 1]
        if turned:
            first, second = second, first
        return (
            pltpu.make_async_copy(first, base.at[i], base_sem.at[i]),
            pltpu.make_async_copy(second, other.at[i], other_sem.at[i, 0]),
        )

    def straight(shift):
        moved = z + shift
        return ((moved + 8) & 7) >> 2 == z >> 2

    for i, shift in enumerate(shifts):
        for turned in (False, True):

            @pl.when(straight(shift) != turned)
            def _():
                for copy in fetch(i, turned):
                    copy.start()

    for i, shift in enumerate(shifts):
        low = (z + shift + 8) & 3
        for copy in fetch(i, False):
            copy.wait()

        def column(c, carry):
            start = pl.multiple_of(c * COLS, COLS)
            picks = one_hot(maps[low, :, pl.ds(start, COLS)], length, COLS)
            turned = jnp.dot(other[i], picks, preferred_element_type=jnp.float32)
            mine = base[i, :, pl.ds(start, COLS)].astype(jnp.float32)
            folded[i, :, pl.ds(start, COLS)] = ((mine + sign * turned) * 0.5).astype(jnp.bfloat16)
            return carry

        lax.fori_loop(0, length // COLS, column, 0)

        for receiver in range(8):
            for half in range(2):
                segment = facts[1 + receiver * 8 + low + 4 * half]

                @pl.when(segment >= 0)
                def _():
                    start = pl.multiple_of(segment * 128, 128)
                    pltpu.make_async_copy(
                        folded.at[i, :, pl.ds(start, 128)],
                        out.at[receiver, 2 * (shift & 3) + half],
                        out_sem.at[i, receiver, half],
                    ).start()

    for i, shift in enumerate(shifts):
        low = (z + shift + 8) & 3
        for receiver in range(8):
            for half in range(2):

                @pl.when(facts[1 + receiver * 8 + low + 4 * half] >= 0)
                def _():
                    pltpu.make_async_copy(
                        folded.at[i, :, pl.ds(0, 128)],
                        out.at[receiver, 2 * (shift & 3) + half],
                        out_sem.at[i, receiver, half],
                    ).wait()


def fold(shifts, facts, maps, tiles, before):
    rows, length = tiles[0].shape
    count = len(shifts)
    whole = pltpu.VMEM((count, rows, length), jnp.bfloat16)
    return pl.pallas_call(
        functools.partial(fold_body, shifts),
        in_specs=[pl.BlockSpec(memory_space=pltpu.SMEM), pl.BlockSpec(memory_space=pltpu.VMEM)]
        + [pl.BlockSpec(memory_space=pl.ANY)] * (len(tiles) + len(before)),
        out_specs=pl.BlockSpec(memory_space=pl.ANY),
        out_shape=pltpu.HBM((8, 8, rows, 128), jnp.bfloat16),
        scratch_shapes=[
            whole,
            whole,
            whole,
            pltpu.SemaphoreType.DMA((count,)),
            pltpu.SemaphoreType.DMA((count, 2)),
            pltpu.SemaphoreType.DMA((count, 8, 2)),
        ],
        compiler_params=pltpu.CompilerParams(vmem_limit_bytes=VMEM),
        cost_estimate=pl.CostEstimate(
            flops=2 * count * rows * length * length,
            bytes_accessed=count * rows * (4 * length + 16 * 256),
            transcendentals=0,
        ),
        input_output_aliases={2 + len(tiles): 0} if before else {},
        name="fold",
    )(facts, maps, *tiles, *before)


def nothing(*refs):
    pass


def joined(block, others, kind=jax.ShapeDtypeStruct):
    held = pl.BlockSpec(memory_space=pl.ANY)
    return pl.pallas_call(
        nothing,
        in_specs=[held] * (1 + len(others)),
        out_specs=held,
        out_shape=kind(block.shape, block.dtype),
        input_output_aliases={0: 0},
        compiler_params=pltpu.CompilerParams(vmem_limit_bytes=VMEM),
        name="joined",
    )(block, *others)


def ladder_body(facts, send_map, blocks, received, ladder, sent, operand, rounded, sem):
    step = pl.program_id(0)
    slots = operand.shape[1] // 128
    length = rounded.shape[1]

    @pl.when(step == 0)
    def _():
        def place(k):
            return operand.at[:, pl.ds(k * 128, 128)]

        def copy(k):
            tile = facts[1 + k]
            z, ket = tile >> 3, tile & 7
            slot = 2 * ((z - facts[0] + 8) & 3) + (z >> 2)
            return pltpu.make_async_copy(received.at[ket, slot], place(k), sem.at[k])

        for k in range(slots):
            copy(k).start()
        for k in range(slots):
            copy(k).wait()

    total = jnp.dot(operand[...], blocks[...], preferred_element_type=jnp.float32)
    ladder[...] = total
    rounded[:, pl.ds(pl.multiple_of(step * COLS, COLS), COLS)] = total.astype(jnp.bfloat16)

    @pl.when(step == pl.num_programs(0) - 1)
    def _():
        def column(c, carry):
            start = pl.multiple_of(c * COLS, COLS)
            picks = one_hot(send_map[:, pl.ds(start, COLS)], length, COLS)
            moved = jnp.dot(rounded[...], picks, preferred_element_type=jnp.float32)
            sent[:, pl.ds(start, COLS)] = moved.astype(jnp.bfloat16)
            return carry

        lax.fori_loop(0, length // COLS, column, 0)


def ladder_of(facts, send_map, blocks, received):
    depth, length = blocks.shape
    rows = received.shape[2]
    return pl.pallas_call(
        ladder_body,
        grid=(length // COLS,),
        in_specs=[
            pl.BlockSpec(memory_space=pltpu.SMEM),
            pl.BlockSpec((1, length), lambda n: (0, 0)),
            pl.BlockSpec((depth, COLS), lambda n: (0, n)),
            pl.BlockSpec(memory_space=pl.ANY),
        ],
        out_specs=[
            pl.BlockSpec((rows, COLS), lambda n: (0, n)),
            pl.BlockSpec((rows, length), lambda n: (0, 0)),
        ],
        out_shape=[
            pltpu.HBM((rows, length), jnp.float32),
            jax.ShapeDtypeStruct((rows, length), jnp.bfloat16),
        ],
        scratch_shapes=[
            pltpu.VMEM((rows, depth), jnp.bfloat16),
            pltpu.VMEM((rows, length), jnp.bfloat16),
            pltpu.SemaphoreType.DMA((depth // 128,)),
        ],
        compiler_params=pltpu.CompilerParams(
            vmem_limit_bytes=VMEM, dimension_semantics=("arbitrary",)
        ),
        cost_estimate=pl.CostEstimate(
            flops=2 * rows * depth * length,
            bytes_accessed=2 * depth * (rows + length),
            transcendentals=0,
        ),
        name="ladder",
    )(facts, send_map, blocks, received)


def shifted(block, by):
    return lax.ppermute(block, "bra", [(i, (i + by) % 8) for i in range(8)])


def energies(table, indices):
    number = lax.broadcasted_iota(jnp.int32, (table.shape[0], 1), 0)
    return jnp.sum(jnp.where(number == indices[None, :], table[:, None], 0.0), axis=0)


def local(
    amplitudes, integrals, screen_list, block_owner, mirror_map, pair_virt, vir_energy, pair_energy
):
    z, ket = lax.axis_index("bra"), lax.axis_index("ket")
    own = amplitudes[:, 0, :]
    rows, length = own.shape
    all_blocks = lax.all_gather(integrals[0], "pair", axis=0, tiled=True).reshape(-1, length)

    wanted = lax.all_gather(block_owner[0] * 16 + screen_list[0], "ket", axis=0)
    served = jnp.arange(8, dtype=jnp.int32) * 8 + ket
    match = (wanted >> 4)[:, None, :] == served[None, :, None]
    asked = jnp.max(jnp.where(match, wanted[:, None, :] & 15, -1), axis=2)
    fold_facts = jnp.concatenate([z.astype(jnp.int32)[None], asked.reshape(-1)])
    ladder_facts = jnp.concatenate([z.astype(jnp.int32)[None], block_owner[0]])
    grid_maps = mirror_map.reshape(2, 4, 8, length)
    half_maps = lax.dynamic_index_in_dim(grid_maps, z >> 2, 0, keepdims=False)
    maps = lax.dynamic_index_in_dim(half_maps, ket, 1, keepdims=True)
    send_map = lax.dynamic_index_in_dim(mirror_map, ((z + 4) & 7) * 8 + ket, 0, keepdims=True)

    direction = jnp.where(z >= 4, 1.0, -1.0).astype(jnp.float32)
    first = energies(vir_energy, pair_virt[0, 0])
    second = energies(vir_energy, pair_virt[0, 1])
    ends = (0, 224, rows)
    parts = [own[low:high] for low, high in zip(ends, ends[1:])]
    rings = []
    for i, part in enumerate(parts):
        if i:
            part = joined(part, rings[i - 1][2], pltpu.HBM)
        up1, down1 = shifted(part, -1), shifted(part, 1)
        up2, down2 = shifted(up1, -1), shifted(down1, 1)
        up3, down3 = shifted(up2, -1), shifted(down2, 1)
        cut = part.shape[0] // 2
        far = (shifted(up3[:cut], -1), shifted(down3[cut:], 1))
        rings.append(((up1, down1), (up2, down2), (up3, down3), far))
    updated = []
    for i, part in enumerate(parts):
        one, two, three, far = rings[i]
        slots = fold((2,), fold_facts, maps, two, ())
        slots = fold((1, 3), fold_facts, maps, (one[0], three[1], three[0], one[1]), (slots,))
        slots = fold((0,), fold_facts, maps, (part, *far), (slots,))
        if i + 1 < len(parts):
            slots = joined(slots, rings[i + 1][0], pltpu.HBM)
        received = lax.all_to_all(slots, "ket", split_axis=0, concat_axis=0, tiled=True)
        ladder, sent = ladder_of(ladder_facts, send_map, all_blocks, received)
        partner = shifted(sent, 4)
        residual = ladder + direction * partner.astype(jnp.float32)
        occupied = pair_energy[ends[i] : ends[i + 1]]
        denominator = occupied[:, None] - first[None, :] - second[None, :]
        fresh = part.astype(jnp.float32) + residual / denominator
        updated.append(fresh.astype(jnp.bfloat16))
    return jnp.concatenate(updated, axis=0)[:, None, :]


def solution(mesh):
    placed = (
        P("pair", ("bra", "ket"), None),
        P(("bra", "ket"), "pair", None, None),
        P(("bra", "ket"), None),
        P(("bra", "ket"), None),
        P(),
        P(("bra", "ket"), None, None),
        P(),
        P("pair"),
    )
    return jax.shard_map(
        local,
        mesh=mesh,
        in_specs=placed,
        out_specs=P("pair", ("bra", "ket"), None),
        check_vma=False,
    )
```

```python
import functools

import jax
import jax.numpy as jnp
from jax import lax
from jax.experimental import pallas as pl
from jax.experimental.pallas import tpu as pltpu
from jax.sharding import PartitionSpec as P

COLS = 256
VMEM = 40 * 1024 * 1024


def one_hot(row, length, width):
    number = lax.broadcasted_iota(jnp.int32, (length, width), 0)
    return jnp.where(number == row, 1.0, 0.0).astype(jnp.bfloat16)


def fold_body(shifts, facts, maps, *refs):
    count = len(shifts)
    tiles = refs[: 3 if shifts == (0,) else 2 * count]
    out, done, base, other, folded, base_sem, other_sem, out_sem = refs[-8:]
    done[0] = 0
    z = facts[0]
    sign = jnp.where(z < 4, 1.0, -1.0).astype(jnp.float32)
    rows, length = folded.shape[1:]

    def fetch(i, turned):
        if shifts[i] == 0:
            cut = tiles[1].shape[0]
            return (
                pltpu.make_async_copy(tiles[0], base.at[i], base_sem.at[i]),
                pltpu.make_async_copy(tiles[1], other.at[i, pl.ds(0, cut)], other_sem.at[i, 0]),
                pltpu.make_async_copy(tiles[2], other.at[i, pl.ds(cut, cut)], other_sem.at[i, 1]),
            )
        first, second = tiles[2 * i], tiles[2 * i + 1]
        if turned:
            first, second = second, first
        return (
            pltpu.make_async_copy(first, base.at[i], base_sem.at[i]),
            pltpu.make_async_copy(second, other.at[i], other_sem.at[i, 0]),
        )

    def straight(shift):
        moved = z + shift
        return ((moved + 8) & 7) >> 2 == z >> 2

    for i, shift in enumerate(shifts):
        for turned in (False, True):

            @pl.when(straight(shift) != turned)
            def _():
                for copy in fetch(i, turned):
                    copy.start()

    for i, shift in enumerate(shifts):
        low = (z + shift + 8) & 3
        for copy in fetch(i, False):
            copy.wait()

        def column(c, carry):
            start = pl.multiple_of(c * COLS, COLS)
            picks = one_hot(maps[low, :, pl.ds(start, COLS)], length, COLS)
            turned = jnp.dot(other[i], picks, preferred_element_type=jnp.float32)
            mine = base[i, :, pl.ds(start, COLS)].astype(jnp.float32)
            folded[i, :, pl.ds(start, COLS)] = ((mine + sign * turned) * 0.5).astype(jnp.bfloat16)
            return carry

        lax.fori_loop(0, length // COLS, column, 0, unroll=True)

        for receiver in range(8):
            for half in range(2):
                segment = facts[1 + receiver * 8 + low + 4 * half]

                @pl.when(segment >= 0)
                def _():
                    start = pl.multiple_of(segment * 128, 128)
                    pltpu.make_async_copy(
                        folded.at[i, :, pl.ds(start, 128)],
                        out.at[receiver, 2 * (shift & 3) + half],
                        out_sem.at[i, receiver, half],
                    ).start()

    for i, shift in enumerate(shifts):
        low = (z + shift + 8) & 3
        for receiver in range(8):
            for half in range(2):

                @pl.when(facts[1 + receiver * 8 + low + 4 * half] >= 0)
                def _():
                    pltpu.make_async_copy(
                        folded.at[i, :, pl.ds(0, 128)],
                        out.at[receiver, 2 * (shift & 3) + half],
                        out_sem.at[i, receiver, half],
                    ).wait()


def fold(shifts, facts, maps, tiles, before):
    rows, length = tiles[0].shape
    count = len(shifts)
    whole = pltpu.VMEM((count, rows, length), jnp.bfloat16)
    return pl.pallas_call(
        functools.partial(fold_body, shifts),
        in_specs=[pl.BlockSpec(memory_space=pltpu.SMEM), pl.BlockSpec(memory_space=pltpu.VMEM)]
        + [pl.BlockSpec(memory_space=pl.ANY)] * (len(tiles) + len(before)),
        out_specs=[pl.BlockSpec(memory_space=pl.ANY), pl.BlockSpec(memory_space=pltpu.SMEM)],
        out_shape=[
            pltpu.HBM((8, 8, rows, 128), jnp.bfloat16),
            jax.ShapeDtypeStruct((1,), jnp.int32),
        ],
        scratch_shapes=[
            whole,
            whole,
            whole,
            pltpu.SemaphoreType.DMA((count,)),
            pltpu.SemaphoreType.DMA((count, 2)),
            pltpu.SemaphoreType.DMA((count, 8, 2)),
        ],
        compiler_params=pltpu.CompilerParams(vmem_limit_bytes=VMEM),
        cost_estimate=pl.CostEstimate(
            flops=2 * count * rows * length * length,
            bytes_accessed=count * rows * (4 * length + 16 * 256),
            transcendentals=0,
        ),
        input_output_aliases={2 + len(tiles): 0} if before else {},
        name="fold",
    )(facts, maps, *tiles, *before)


def nothing(*refs):
    pass


def joined(block, others, kind=jax.ShapeDtypeStruct):
    held = pl.BlockSpec(memory_space=pl.ANY)
    return pl.pallas_call(
        nothing,
        in_specs=[held] * (1 + len(others)),
        out_specs=held,
        out_shape=kind(block.shape, block.dtype),
        input_output_aliases={0: 0},
        compiler_params=pltpu.CompilerParams(vmem_limit_bytes=VMEM),
        name="joined",
    )(block, *others)


def halves_body(first, second, _, first_out, second_out, sem):
    cut = first_out.shape[0]
    copies = (
        pltpu.make_async_copy(first.at[pl.ds(0, cut)], first_out, sem.at[0]),
        pltpu.make_async_copy(second.at[pl.ds(cut, cut)], second_out, sem.at[1]),
    )
    for copy in copies:
        copy.start()
    for copy in copies:
        copy.wait()


def halves(first, second, after):
    rows, length = first.shape
    held = pl.BlockSpec(memory_space=pl.ANY)
    part = jax.ShapeDtypeStruct((rows // 2, length), first.dtype)
    return pl.pallas_call(
        halves_body,
        in_specs=[held] * 3,
        out_specs=[held] * 2,
        out_shape=[part] * 2,
        scratch_shapes=[pltpu.SemaphoreType.DMA((2,))],
        compiler_params=pltpu.CompilerParams(vmem_limit_bytes=VMEM),
        name="halves",
    )(first, second, after)


def ladder_body(facts, send_map, blocks, received, ladder, sent, operand, rounded, sem):
    step = pl.program_id(0)
    slots = operand.shape[1] // 128
    length = rounded.shape[1]

    @pl.when(step == 0)
    def _():
        def place(k):
            return operand.at[:, pl.ds(k * 128, 128)]

        def copy(k):
            tile = facts[1 + k]
            z, ket = tile >> 3, tile & 7
            slot = 2 * ((z - facts[0] + 8) & 3) + (z >> 2)
            return pltpu.make_async_copy(received.at[ket, slot], place(k), sem.at[k])

        for k in range(slots):
            copy(k).start()
        for k in range(slots):
            copy(k).wait()

    total = jnp.dot(operand[...], blocks[...], preferred_element_type=jnp.float32)
    ladder[...] = total
    rounded[:, pl.ds(pl.multiple_of(step * COLS, COLS), COLS)] = total.astype(jnp.bfloat16)

    @pl.when(step == pl.num_programs(0) - 1)
    def _():
        def column(c, carry):
            start = pl.multiple_of(c * COLS, COLS)
            picks = one_hot(send_map[:, pl.ds(start, COLS)], length, COLS)
            moved = jnp.dot(rounded[...], picks, preferred_element_type=jnp.float32)
            sent[:, pl.ds(start, COLS)] = moved.astype(jnp.bfloat16)
            return carry

        lax.fori_loop(0, length // COLS, column, 0, unroll=True)


def ladder_of(facts, send_map, blocks, received):
    depth, length = blocks.shape
    rows = received.shape[2]
    return pl.pallas_call(
        ladder_body,
        grid=(length // COLS,),
        in_specs=[
            pl.BlockSpec(memory_space=pltpu.SMEM),
            pl.BlockSpec((1, length), lambda n: (0, 0)),
            pl.BlockSpec((depth, COLS), lambda n: (0, n)),
            pl.BlockSpec(memory_space=pl.ANY),
        ],
        out_specs=[
            pl.BlockSpec((rows, COLS), lambda n: (0, n)),
            pl.BlockSpec((rows, length), lambda n: (0, 0)),
        ],
        out_shape=[
            pltpu.HBM((rows, length), jnp.float32),
            jax.ShapeDtypeStruct((rows, length), jnp.bfloat16),
        ],
        scratch_shapes=[
            pltpu.VMEM((rows, depth), jnp.bfloat16),
            pltpu.VMEM((rows, length), jnp.bfloat16),
            pltpu.SemaphoreType.DMA((depth // 128,)),
        ],
        compiler_params=pltpu.CompilerParams(
            vmem_limit_bytes=VMEM, dimension_semantics=("arbitrary",)
        ),
        cost_estimate=pl.CostEstimate(
            flops=2 * rows * depth * length,
            bytes_accessed=2 * depth * (rows + length),
            transcendentals=0,
        ),
        name="ladder",
    )(facts, send_map, blocks, received)


def update_body(low, *refs):
    own, ladder, partner, direction, occupied, virtual, out = refs[:7] if len(refs) == 7 else refs[:6] + refs[7:]
    residual = ladder[...] + direction[0] * partner[...].astype(jnp.float32)
    denominator = occupied[...] - virtual[0:1, :] - virtual[1:2, :]
    out[...] = (own[...].astype(jnp.float32) + residual / denominator).astype(jnp.bfloat16)


def update(low, own, ladder, partner, direction, occupied, virtual, before):
    rows, length = ladder.shape
    step = 32

    def chunk(width):
        return pl.BlockSpec((step, width), lambda n: (n, 0))

    def whole(width):
        return pl.BlockSpec((step, width), lambda n: (n + low // step, 0))

    return pl.pallas_call(
        functools.partial(update_body, low),
        grid=(rows // step,),
        in_specs=[
            whole(length),
            chunk(length),
            chunk(length),
            pl.BlockSpec(memory_space=pltpu.SMEM),
            whole(1),
            pl.BlockSpec((2, length), lambda n: (0, 0)),
        ]
        + [pl.BlockSpec(memory_space=pl.ANY)] * len(before),
        out_specs=whole(length),
        out_shape=jax.ShapeDtypeStruct(own.shape, jnp.bfloat16),
        input_output_aliases={6: 0} if before else {},
        compiler_params=pltpu.CompilerParams(
            vmem_limit_bytes=VMEM, dimension_semantics=("arbitrary",)
        ),
        cost_estimate=pl.CostEstimate(
            flops=8 * rows * length, bytes_accessed=10 * rows * length, transcendentals=0
        ),
        name="update",
    )(own, ladder, partner, direction, occupied, virtual, *before)


def shifted(block, by):
    return lax.ppermute(block, "bra", [(i, (i + by) % 8) for i in range(8)])


def energies(table, indices):
    number = lax.broadcasted_iota(jnp.int32, (table.shape[0], 1), 0)
    return jnp.sum(jnp.where(number == indices[None, :], table[:, None], 0.0), axis=0)


def local(
    amplitudes, integrals, screen_list, block_owner, mirror_map, pair_virt, vir_energy, pair_energy
):
    z, ket = lax.axis_index("bra"), lax.axis_index("ket")
    own = amplitudes[:, 0, :]
    rows, length = own.shape
    all_blocks = lax.all_gather(integrals[0], "pair", axis=0, tiled=True).reshape(-1, length)

    wanted = lax.all_gather(block_owner[0] * 16 + screen_list[0], "ket", axis=0)
    served = jnp.arange(8, dtype=jnp.int32) * 8 + ket
    match = (wanted >> 4)[:, None, :] == served[None, :, None]
    asked = jnp.max(jnp.where(match, wanted[:, None, :] & 15, -1), axis=2)
    fold_facts = jnp.concatenate([z.astype(jnp.int32)[None], asked.reshape(-1)])
    ladder_facts = jnp.concatenate([z.astype(jnp.int32)[None], block_owner[0]])
    grid_maps = mirror_map.reshape(2, 4, 8, length)
    half_maps = lax.dynamic_index_in_dim(grid_maps, z >> 2, 0, keepdims=False)
    maps = lax.dynamic_index_in_dim(half_maps, ket, 1, keepdims=True)
    send_map = lax.dynamic_index_in_dim(mirror_map, ((z + 4) & 7) * 8 + ket, 0, keepdims=True)

    direction = jnp.where(z >= 4, 1.0, -1.0).astype(jnp.float32)
    first = energies(vir_energy, pair_virt[0, 0])
    second = energies(vir_energy, pair_virt[0, 1])
    virtual = jnp.stack([first, second])
    ends = (0, 224, rows)
    steps, folds = [], []
    for low, high in zip(ends, ends[1:]):
        part = own[low:high]
        if steps:
            part = joined(part, steps[-1][2], pltpu.HBM)
        one = (shifted(part, -1), shifted(part, 1))
        two = (shifted(one[0], -1), shifted(one[1], 1))
        slots, done = fold((2,), fold_facts, maps, two, ())
        three = (shifted(two[0], -1), shifted(two[1], 1))
        upper, lower = halves(*three, done if steps else fold_facts)
        far = (shifted(upper, -1), shifted(lower, 1))
        odd = (one[0], three[1], three[0], one[1])
        slots, _ = fold((1, 3), fold_facts, maps, odd, (slots,))
        steps.append((part, one, two, far))
        folds.append(slots)
    fresh = ()
    for i, (part, one, two, far) in enumerate(steps):
        slots, _ = fold((0,), fold_facts, maps, (part, *far), (folds[i],))
        if i + 1 < len(steps):
            slots = joined(slots, steps[i + 1][2], pltpu.HBM)
        received = lax.all_to_all(slots, "ket", split_axis=0, concat_axis=0, tiled=True)
        ladder, sent = ladder_of(ladder_facts, send_map, all_blocks, received)
        partner = shifted(sent, 4)
        fresh = update(ends[i], own, ladder, partner, direction[None], pair_energy[:, None], virtual, fresh)
        fresh = (fresh,)
    return fresh[0][:, None, :]


def solution(mesh):
    placed = (
        P("pair", ("bra", "ket"), None),
        P(("bra", "ket"), "pair", None, None),
        P(("bra", "ket"), None),
        P(("bra", "ket"), None),
        P(),
        P(("bra", "ket"), None, None),
        P(),
        P("pair"),
    )
    return jax.shard_map(
        local,
        mesh=mesh,
        in_specs=placed,
        out_specs=P("pair", ("bra", "ket"), None),
        check_vma=False,
    )
```

```python
import functools

import jax
import jax.numpy as jnp
from jax import lax
from jax.experimental import pallas as pl
from jax.experimental.pallas import tpu as pltpu
from jax.sharding import PartitionSpec as P

COLS = 256
VMEM = 40 * 1024 * 1024


def one_hot(row, length, width):
    number = lax.broadcasted_iota(jnp.int32, (length, width), 0)
    return jnp.where(number == row, 1.0, 0.0).astype(jnp.bfloat16)


def fold_body(shifts, facts, maps, *refs):
    count = len(shifts)
    tiles = refs[: 3 if shifts == (0,) else 2 * count]
    out, done, base, other, folded, base_sem, other_sem, out_sem = refs[-8:]
    done[0] = 0
    z = facts[0]
    sign = jnp.where(z < 4, 1.0, -1.0).astype(jnp.float32)
    rows, length = folded.shape[1:]

    def fetch(i, turned):
        if shifts[i] == 0:
            cut = tiles[1].shape[0]
            return (
                pltpu.make_async_copy(tiles[0], base.at[i], base_sem.at[i]),
                pltpu.make_async_copy(tiles[1], other.at[i, pl.ds(0, cut)], other_sem.at[i, 0]),
                pltpu.make_async_copy(tiles[2], other.at[i, pl.ds(cut, cut)], other_sem.at[i, 1]),
            )
        first, second = tiles[2 * i], tiles[2 * i + 1]
        if turned:
            first, second = second, first
        return (
            pltpu.make_async_copy(first, base.at[i], base_sem.at[i]),
            pltpu.make_async_copy(second, other.at[i], other_sem.at[i, 0]),
        )

    def straight(shift):
        moved = z + shift
        return ((moved + 8) & 7) >> 2 == z >> 2

    for i, shift in enumerate(shifts):
        for turned in (False, True):

            @pl.when(straight(shift) != turned)
            def _():
                for copy in fetch(i, turned):
                    copy.start()

    for i, shift in enumerate(shifts):
        low = (z + shift + 8) & 3
        for copy in fetch(i, False):
            copy.wait()

        def column(c, carry):
            start = pl.multiple_of(c * COLS, COLS)
            picks = one_hot(maps[low, :, pl.ds(start, COLS)], length, COLS)
            turned = jnp.dot(other[i], picks, preferred_element_type=jnp.float32)
            mine = base[i, :, pl.ds(start, COLS)].astype(jnp.float32)
            folded[i, :, pl.ds(start, COLS)] = ((mine + sign * turned) * 0.5).astype(jnp.bfloat16)
            return carry

        lax.fori_loop(0, length // COLS, column, 0, unroll=True)

        for receiver in range(8):
            for half in range(2):
                segment = facts[1 + receiver * 8 + low + 4 * half]

                @pl.when(segment >= 0)
                def _():
                    start = pl.multiple_of(segment * 128, 128)
                    pltpu.make_async_copy(
                        folded.at[i, :, pl.ds(start, 128)],
                        out.at[receiver, 2 * (shift & 3) + half],
                        out_sem.at[i, receiver, half],
                    ).start()

    for i, shift in enumerate(shifts):
        low = (z + shift + 8) & 3
        for receiver in range(8):
            for half in range(2):

                @pl.when(facts[1 + receiver * 8 + low + 4 * half] >= 0)
                def _():
                    pltpu.make_async_copy(
                        folded.at[i, :, pl.ds(0, 128)],
                        out.at[receiver, 2 * (shift & 3) + half],
                        out_sem.at[i, receiver, half],
                    ).wait()


def fold(shifts, facts, maps, tiles, before):
    rows, length = tiles[0].shape
    count = len(shifts)
    whole = pltpu.VMEM((count, rows, length), jnp.bfloat16)
    return pl.pallas_call(
        functools.partial(fold_body, shifts),
        in_specs=[pl.BlockSpec(memory_space=pltpu.SMEM), pl.BlockSpec(memory_space=pltpu.VMEM)]
        + [pl.BlockSpec(memory_space=pl.ANY)] * (len(tiles) + len(before)),
        out_specs=[pl.BlockSpec(memory_space=pl.ANY), pl.BlockSpec(memory_space=pltpu.SMEM)],
        out_shape=[
            pltpu.HBM((8, 8, rows, 128), jnp.bfloat16),
            jax.ShapeDtypeStruct((1,), jnp.int32),
        ],
        scratch_shapes=[
            whole,
            whole,
            whole,
            pltpu.SemaphoreType.DMA((count,)),
            pltpu.SemaphoreType.DMA((count, 2)),
            pltpu.SemaphoreType.DMA((count, 8, 2)),
        ],
        compiler_params=pltpu.CompilerParams(vmem_limit_bytes=VMEM),
        cost_estimate=pl.CostEstimate(
            flops=2 * count * rows * length * length,
            bytes_accessed=count * rows * (4 * length + 16 * 256),
            transcendentals=0,
        ),
        input_output_aliases={2 + len(tiles): 0} if before else {},
        name="fold",
    )(facts, maps, *tiles, *before)


def nothing(*refs):
    pass


def joined(block, others, kind=jax.ShapeDtypeStruct):
    held = pl.BlockSpec(memory_space=pl.ANY)
    return pl.pallas_call(
        nothing,
        in_specs=[held] * (1 + len(others)),
        out_specs=held,
        out_shape=kind(block.shape, block.dtype),
        input_output_aliases={0: 0},
        compiler_params=pltpu.CompilerParams(vmem_limit_bytes=VMEM),
        name="joined",
    )(block, *others)


def halves_body(first, second, _, first_out, second_out, sem):
    cut = first_out.shape[0]
    copies = (
        pltpu.make_async_copy(first.at[pl.ds(0, cut)], first_out, sem.at[0]),
        pltpu.make_async_copy(second.at[pl.ds(cut, cut)], second_out, sem.at[1]),
    )
    for copy in copies:
        copy.start()
    for copy in copies:
        copy.wait()


def halves(first, second, after):
    rows, length = first.shape
    held = pl.BlockSpec(memory_space=pl.ANY)
    part = jax.ShapeDtypeStruct((rows // 2, length), first.dtype)
    return pl.pallas_call(
        halves_body,
        in_specs=[held] * 3,
        out_specs=[held] * 2,
        out_shape=[part] * 2,
        scratch_shapes=[pltpu.SemaphoreType.DMA((2,))],
        compiler_params=pltpu.CompilerParams(vmem_limit_bytes=VMEM),
        name="halves",
    )(first, second, after)


def ladder_body(facts, send_map, blocks, received, ladder, sent, operand, rounded, held, sem, held_sem):
    length = rounded.shape[1]
    parts = held_sem.shape[0]
    depth = held.shape[0] // parts

    def place(k):
        tile = facts[1 + k]
        z, ket = tile >> 3, tile & 7
        slot = 2 * ((z - facts[0] + 8) & 3) + (z >> 2)
        where = operand.at[:, pl.ds(k * 128, 128)]
        return pltpu.make_async_copy(received.at[ket, slot], where, sem.at[k])

    def bring(i):
        rows = pl.ds(i * depth, depth)
        return pltpu.make_async_copy(blocks.at[rows], held.at[rows], held_sem.at[i])

    each = depth // 128
    for i in range(parts):
        for k in range(i * each, (i + 1) * each):
            place(k).start()
        bring(i).start()
    for i in range(parts):
        for k in range(i * each, (i + 1) * each):
            place(k).wait()
        bring(i).wait()
        rows = slice(i * depth, (i + 1) * depth)
        for low in range(0, length, COLS):
            columns = slice(low, low + COLS)
            total = jnp.dot(operand[:, rows], held[rows, columns], preferred_element_type=jnp.float32)
            if i:
                total += ladder[:, columns]
            ladder[:, columns] = total
            if i == parts - 1:
                rounded[:, columns] = total.astype(jnp.bfloat16)
    for low in range(0, length, COLS):
        columns = slice(low, low + COLS)
        picks = one_hot(send_map[:, columns], length, COLS)
        moved = jnp.dot(rounded[...], picks, preferred_element_type=jnp.float32)
        sent[:, columns] = moved.astype(jnp.bfloat16)


def ladder_of(facts, send_map, blocks, received):
    depth, length = blocks.shape
    rows = received.shape[2]
    vmem = pl.BlockSpec(memory_space=pltpu.VMEM)
    return pl.pallas_call(
        ladder_body,
        in_specs=[
            pl.BlockSpec(memory_space=pltpu.SMEM),
            vmem,
            pl.BlockSpec(memory_space=pl.ANY),
            pl.BlockSpec(memory_space=pl.ANY),
        ],
        out_specs=[vmem, vmem],
        out_shape=[
            jax.ShapeDtypeStruct((rows, length), jnp.float32),
            jax.ShapeDtypeStruct((rows, length), jnp.bfloat16),
        ],
        scratch_shapes=[
            pltpu.VMEM((rows, depth), jnp.bfloat16),
            pltpu.VMEM((rows, length), jnp.bfloat16),
            pltpu.VMEM((depth, length), jnp.bfloat16),
            pltpu.SemaphoreType.DMA((depth // 128,)),
            pltpu.SemaphoreType.DMA((4,)),
        ],
        compiler_params=pltpu.CompilerParams(vmem_limit_bytes=VMEM),
        cost_estimate=pl.CostEstimate(
            flops=2 * rows * depth * length,
            bytes_accessed=2 * depth * (rows + length),
            transcendentals=0,
        ),
        name="ladder",
    )(facts, send_map, blocks, received)


def update_body(low, *refs):
    own, ladder, partner, direction, occupied, virtual, out = refs[:7] if len(refs) == 7 else refs[:6] + refs[7:]
    residual = ladder[...] + direction[0] * partner[...].astype(jnp.float32)
    denominator = occupied[...] - virtual[0:1, :] - virtual[1:2, :]
    out[...] = (own[...].astype(jnp.float32) + residual / denominator).astype(jnp.bfloat16)


def update(low, own, ladder, partner, direction, occupied, virtual, before):
    rows, length = ladder.shape
    step = 64

    def chunk(width):
        return pl.BlockSpec((step, width), lambda n: (n, 0))

    def whole(width):
        return pl.BlockSpec((step, width), lambda n: (n + low // step, 0))

    return pl.pallas_call(
        functools.partial(update_body, low),
        grid=(rows // step,),
        in_specs=[
            whole(length),
            chunk(length),
            chunk(length),
            pl.BlockSpec(memory_space=pltpu.SMEM),
            whole(1),
            pl.BlockSpec((2, length), lambda n: (0, 0)),
        ]
        + [pl.BlockSpec(memory_space=pl.ANY)] * len(before),
        out_specs=whole(length),
        out_shape=jax.ShapeDtypeStruct(own.shape, jnp.bfloat16),
        input_output_aliases={6: 0} if before else {},
        compiler_params=pltpu.CompilerParams(
            vmem_limit_bytes=VMEM, dimension_semantics=("arbitrary",)
        ),
        cost_estimate=pl.CostEstimate(
            flops=8 * rows * length, bytes_accessed=10 * rows * length, transcendentals=0
        ),
        name="update",
    )(own, ladder, partner, direction, occupied, virtual, *before)


def shifted(block, by):
    return lax.ppermute(block, "bra", [(i, (i + by) % 8) for i in range(8)])


def energies(table, indices):
    number = lax.broadcasted_iota(jnp.int32, (table.shape[0], 1), 0)
    return jnp.sum(jnp.where(number == indices[None, :], table[:, None], 0.0), axis=0)


def local(
    amplitudes, integrals, screen_list, block_owner, mirror_map, pair_virt, vir_energy, pair_energy
):
    z, ket = lax.axis_index("bra"), lax.axis_index("ket")
    own = amplitudes[:, 0, :]
    rows, length = own.shape
    all_blocks = lax.all_gather(integrals[0], "pair", axis=0, tiled=True).reshape(-1, length)

    wanted = lax.all_gather(block_owner[0] * 16 + screen_list[0], "ket", axis=0)
    served = jnp.arange(8, dtype=jnp.int32) * 8 + ket
    match = (wanted >> 4)[:, None, :] == served[None, :, None]
    asked = jnp.max(jnp.where(match, wanted[:, None, :] & 15, -1), axis=2)
    fold_facts = jnp.concatenate([z.astype(jnp.int32)[None], asked.reshape(-1)])
    ladder_facts = jnp.concatenate([z.astype(jnp.int32)[None], block_owner[0]])
    grid_maps = mirror_map.reshape(2, 4, 8, length)
    half_maps = lax.dynamic_index_in_dim(grid_maps, z >> 2, 0, keepdims=False)
    maps = lax.dynamic_index_in_dim(half_maps, ket, 1, keepdims=True)
    send_map = lax.dynamic_index_in_dim(mirror_map, ((z + 4) & 7) * 8 + ket, 0, keepdims=True)

    direction = jnp.where(z >= 4, 1.0, -1.0).astype(jnp.float32)
    first = energies(vir_energy, pair_virt[0, 0])
    second = energies(vir_energy, pair_virt[0, 1])
    virtual = jnp.stack([first, second])
    ends = (0, 192, rows)
    steps, folds = [], []
    for low, high in zip(ends, ends[1:]):
        part = own[low:high]
        if steps:
            part = joined(part, steps[-1][2], pltpu.HBM)
        one = (shifted(part, -1), shifted(part, 1))
        two = (shifted(one[0], -1), shifted(one[1], 1))
        slots, done = fold((2,), fold_facts, maps, two, ())
        three = (shifted(two[0], -1), shifted(two[1], 1))
        upper, lower = halves(*three, done if steps else fold_facts)
        far = (shifted(upper, -1), shifted(lower, 1))
        odd = (one[0], three[1], three[0], one[1])
        slots, _ = fold((1, 3), fold_facts, maps, odd, (slots,))
        steps.append((part, one, three, far))
        folds.append(slots)
    fresh = ()
    for i, (part, one, three, far) in enumerate(steps):
        slots, _ = fold((0,), fold_facts, maps, (part, *far), (folds[i],))
        if i + 1 < len(steps):
            slots = joined(slots, steps[i + 1][1], pltpu.HBM)
        received = lax.all_to_all(slots, "ket", split_axis=0, concat_axis=0, tiled=True)
        ladder, sent = ladder_of(ladder_facts, send_map, all_blocks, received)
        partner = shifted(sent, 4)
        fresh = update(ends[i], own, ladder, partner, direction[None], pair_energy[:, None], virtual, fresh)
        fresh = (fresh,)
    return fresh[0][:, None, :]


def solution(mesh):
    placed = (
        P("pair", ("bra", "ket"), None),
        P(("bra", "ket"), "pair", None, None),
        P(("bra", "ket"), None),
        P(("bra", "ket"), None),
        P(),
        P(("bra", "ket"), None, None),
        P(),
        P("pair"),
    )
    return jax.shard_map(
        local,
        mesh=mesh,
        in_specs=placed,
        out_specs=P("pair", ("bra", "ket"), None),
        check_vma=False,
    )
```

```python
import functools
import math

import jax
import jax.numpy as jnp
from jax import lax
from jax.experimental import pallas as pl
from jax.experimental.pallas import tpu as pltpu
from jax.sharding import PartitionSpec as P

COLS = 256
VMEM = 40 * 1024 * 1024


def one_hot(row, length, width):
    number = lax.broadcasted_iota(jnp.int32, (length, width), 0)
    return jnp.where(number == row, 1.0, 0.0).astype(jnp.bfloat16)


def fold_body(shifts, pieces, facts, maps, *refs):
    count = len(shifts)
    tiles = refs[: 3 if shifts == (0,) else 2 * count]
    done, base, other, folded, base_sem, other_sem, out_sem = refs[-7:]
    outs = refs[-7 - len(pieces) : -7]
    done[0] = 0
    z = facts[0]
    sign = jnp.where(z < 4, 1.0, -1.0).astype(jnp.float32)
    rows, length = folded.shape[1:]

    def fetch(i, turned):
        if shifts[i] == 0:
            cut = tiles[1].shape[0]
            return (
                pltpu.make_async_copy(tiles[0], base.at[i], base_sem.at[i]),
                pltpu.make_async_copy(tiles[1], other.at[i, pl.ds(0, cut)], other_sem.at[i, 0]),
                pltpu.make_async_copy(tiles[2], other.at[i, pl.ds(cut, cut)], other_sem.at[i, 1]),
            )
        first, second = tiles[2 * i], tiles[2 * i + 1]
        if turned:
            first, second = second, first
        return (
            pltpu.make_async_copy(first, base.at[i], base_sem.at[i]),
            pltpu.make_async_copy(second, other.at[i], other_sem.at[i, 0]),
        )

    def straight(shift):
        moved = z + shift
        return ((moved + 8) & 7) >> 2 == z >> 2

    for i, shift in enumerate(shifts):
        for turned in (False, True):

            @pl.when(straight(shift) != turned)
            def _():
                for copy in fetch(i, turned):
                    copy.start()

    sends = []
    for i, shift in enumerate(shifts):
        low = (z + shift + 8) & 3
        for copy in fetch(i, False):
            copy.wait()

        def column(c, carry):
            start = pl.multiple_of(c * COLS, COLS)
            picks = one_hot(maps[low, :, pl.ds(start, COLS)], length, COLS)
            turned = jnp.dot(other[i], picks, preferred_element_type=jnp.float32)
            mine = base[i, :, pl.ds(start, COLS)].astype(jnp.float32)
            folded[i, :, pl.ds(start, COLS)] = ((mine + sign * turned) * 0.5).astype(jnp.bfloat16)
            return carry

        lax.fori_loop(0, length // COLS, column, 0, unroll=True)

        def send(receiver, half, start, i=i, shift=shift):
            copies, low = [], 0
            for p, (out, count) in enumerate(zip(outs, pieces)):
                source = folded.at[i, pl.ds(low, count), pl.ds(start, 128)]
                place = out.at[receiver, 2 * (shift & 3) + half]
                copies.append(
                    pltpu.make_async_copy(source, place, out_sem.at[i, receiver, 2 * p + half])
                )
                low += count
            return copies

        sends.append(send)
        for receiver in range(8):
            for half in range(2):
                segment = facts[1 + receiver * 8 + low + 4 * half]

                @pl.when(segment >= 0)
                def _():
                    for copy in send(receiver, half, pl.multiple_of(segment * 128, 128)):
                        copy.start()

    for i, shift in enumerate(shifts):
        low = (z + shift + 8) & 3
        for receiver in range(8):
            for half in range(2):

                @pl.when(facts[1 + receiver * 8 + low + 4 * half] >= 0)
                def _():
                    for copy in sends[i](receiver, half, 0):
                        copy.wait()


def fold(shifts, facts, maps, tiles, pieces, before):
    rows, length = tiles[0].shape
    count = len(shifts)
    whole = pltpu.VMEM((count, rows, length), jnp.bfloat16)
    return pl.pallas_call(
        functools.partial(fold_body, shifts, pieces),
        in_specs=[pl.BlockSpec(memory_space=pltpu.SMEM), pl.BlockSpec(memory_space=pltpu.VMEM)]
        + [pl.BlockSpec(memory_space=pl.ANY)] * (len(tiles) + len(before)),
        out_specs=[pl.BlockSpec(memory_space=pl.ANY)] * len(pieces)
        + [pl.BlockSpec(memory_space=pltpu.SMEM)],
        out_shape=[pltpu.HBM((8, 8, piece, 128), jnp.bfloat16) for piece in pieces]
        + [jax.ShapeDtypeStruct((1,), jnp.int32)],
        scratch_shapes=[
            whole,
            whole,
            whole,
            pltpu.SemaphoreType.DMA((count,)),
            pltpu.SemaphoreType.DMA((count, 2)),
            pltpu.SemaphoreType.DMA((count, 8, 2 * len(pieces))),
        ],
        compiler_params=pltpu.CompilerParams(vmem_limit_bytes=VMEM),
        cost_estimate=pl.CostEstimate(
            flops=2 * count * rows * length * length,
            bytes_accessed=count * rows * (4 * length + 16 * 256),
            transcendentals=0,
        ),
        input_output_aliases={2 + len(tiles) + p: p for p in range(len(before))},
        name="fold",
    )(facts, maps, *tiles, *before)


def nothing(*refs):
    pass


def joined(block, others, kind=jax.ShapeDtypeStruct):
    held = pl.BlockSpec(memory_space=pl.ANY)
    return pl.pallas_call(
        nothing,
        in_specs=[held] * (1 + len(others)),
        out_specs=held,
        out_shape=kind(block.shape, block.dtype),
        input_output_aliases={0: 0},
        compiler_params=pltpu.CompilerParams(vmem_limit_bytes=VMEM),
        name="joined",
    )(block, *others)


def halves_body(first, second, _, first_out, second_out, sem):
    cut = first_out.shape[0]
    copies = (
        pltpu.make_async_copy(first.at[pl.ds(0, cut)], first_out, sem.at[0]),
        pltpu.make_async_copy(second.at[pl.ds(cut, cut)], second_out, sem.at[1]),
    )
    for copy in copies:
        copy.start()
    for copy in copies:
        copy.wait()


def halves(first, second, after):
    rows, length = first.shape
    held = pl.BlockSpec(memory_space=pl.ANY)
    part = jax.ShapeDtypeStruct((rows // 2, length), first.dtype)
    return pl.pallas_call(
        halves_body,
        in_specs=[held] * 3,
        out_specs=[held] * 2,
        out_shape=[part] * 2,
        scratch_shapes=[pltpu.SemaphoreType.DMA((2,))],
        compiler_params=pltpu.CompilerParams(vmem_limit_bytes=VMEM),
        name="halves",
    )(first, second, after)


def ladder_body(facts, send_map, blocks, received, ladder, sent, operand, rounded, held, sem, held_sem):
    length = rounded.shape[1]
    parts = held_sem.shape[0]
    depth = held.shape[0] // parts

    def place(k):
        tile = facts[1 + k]
        z, ket = tile >> 3, tile & 7
        slot = 2 * ((z - facts[0] + 8) & 3) + (z >> 2)
        where = operand.at[:, pl.ds(k * 128, 128)]
        return pltpu.make_async_copy(received.at[ket, slot], where, sem.at[k])

    def bring(i):
        rows = pl.ds(i * depth, depth)
        return pltpu.make_async_copy(blocks.at[rows], held.at[rows], held_sem.at[i])

    each = depth // 128
    for i in range(parts):
        for k in range(i * each, (i + 1) * each):
            place(k).start()
        bring(i).start()
    for i in range(parts):
        for k in range(i * each, (i + 1) * each):
            place(k).wait()
        bring(i).wait()
        rows = slice(i * depth, (i + 1) * depth)
        for low in range(0, length, COLS):
            columns = slice(low, low + COLS)
            total = jnp.dot(operand[:, rows], held[rows, columns], preferred_element_type=jnp.float32)
            if i:
                total += ladder[:, columns]
            ladder[:, columns] = total
            if i == parts - 1:
                rounded[:, columns] = total.astype(jnp.bfloat16)
    for low in range(0, length, COLS):
        columns = slice(low, low + COLS)
        picks = one_hot(send_map[:, columns], length, COLS)
        moved = jnp.dot(rounded[...], picks, preferred_element_type=jnp.float32)
        sent[:, columns] = moved.astype(jnp.bfloat16)


def ladder_of(facts, send_map, blocks, received):
    depth, length = blocks.shape
    rows = received.shape[2]
    vmem = pl.BlockSpec(memory_space=pltpu.VMEM)
    return pl.pallas_call(
        ladder_body,
        in_specs=[
            pl.BlockSpec(memory_space=pltpu.SMEM),
            vmem,
            pl.BlockSpec(memory_space=pl.ANY),
            pl.BlockSpec(memory_space=pl.ANY),
        ],
        out_specs=[vmem, vmem],
        out_shape=[
            pltpu.HBM((rows, length), jnp.float32),
            jax.ShapeDtypeStruct((rows, length), jnp.bfloat16),
        ],
        scratch_shapes=[
            pltpu.VMEM((rows, depth), jnp.bfloat16),
            pltpu.VMEM((rows, length), jnp.bfloat16),
            pltpu.VMEM((depth, length), jnp.bfloat16),
            pltpu.SemaphoreType.DMA((depth // 128,)),
            pltpu.SemaphoreType.DMA((4,)),
        ],
        compiler_params=pltpu.CompilerParams(vmem_limit_bytes=60 * 1024 * 1024),
        cost_estimate=pl.CostEstimate(
            flops=2 * rows * depth * length,
            bytes_accessed=2 * depth * (rows + length),
            transcendentals=0,
        ),
        name="ladder",
    )(facts, send_map, blocks, received)


def update_body(low, *refs):
    own, ladder, partner, direction, occupied, virtual, out = refs[:7] if len(refs) == 7 else refs[:6] + refs[7:]
    residual = ladder[...] + direction[0] * partner[...].astype(jnp.float32)
    denominator = occupied[...] - virtual[0:1, :] - virtual[1:2, :]
    out[...] = (own[...].astype(jnp.float32) + residual / denominator).astype(jnp.bfloat16)


def update(low, own, ladder, partner, direction, occupied, virtual, before):
    rows, length = ladder.shape
    step = math.gcd(low, rows) if low else rows // 2

    def chunk(width):
        return pl.BlockSpec((step, width), lambda n: (n, 0))

    def whole(width):
        return pl.BlockSpec((step, width), lambda n: (n + low // step, 0))

    return pl.pallas_call(
        functools.partial(update_body, low),
        grid=(rows // step,),
        in_specs=[
            whole(length),
            chunk(length),
            chunk(length),
            pl.BlockSpec(memory_space=pltpu.SMEM),
            whole(1),
            pl.BlockSpec((2, length), lambda n: (0, 0)),
        ]
        + [pl.BlockSpec(memory_space=pl.ANY)] * len(before),
        out_specs=whole(length),
        out_shape=jax.ShapeDtypeStruct(own.shape, jnp.bfloat16),
        input_output_aliases={6: 0} if before else {},
        compiler_params=pltpu.CompilerParams(
            vmem_limit_bytes=VMEM, dimension_semantics=("arbitrary",)
        ),
        cost_estimate=pl.CostEstimate(
            flops=8 * rows * length, bytes_accessed=10 * rows * length, transcendentals=0
        ),
        name="update",
    )(own, ladder, partner, direction, occupied, virtual, *before)


def shifted(block, by):
    return lax.ppermute(block, "bra", [(i, (i + by) % 8) for i in range(8)])


def energies(table, indices):
    number = lax.broadcasted_iota(jnp.int32, (table.shape[0], 1), 0)
    return jnp.sum(jnp.where(number == indices[None, :], table[:, None], 0.0), axis=0)


def local(
    amplitudes, integrals, screen_list, block_owner, mirror_map, pair_virt, vir_energy, pair_energy
):
    z, ket = lax.axis_index("bra"), lax.axis_index("ket")
    own = amplitudes[:, 0, :]
    rows, length = own.shape
    all_blocks = lax.all_gather(integrals[0], "pair", axis=0, tiled=True).reshape(-1, length)

    wanted = lax.all_gather(block_owner[0] * 16 + screen_list[0], "ket", axis=0)
    served = jnp.arange(8, dtype=jnp.int32) * 8 + ket
    match = (wanted >> 4)[:, None, :] == served[None, :, None]
    asked = jnp.max(jnp.where(match, wanted[:, None, :] & 15, -1), axis=2)
    fold_facts = jnp.concatenate([z.astype(jnp.int32)[None], asked.reshape(-1)])
    ladder_facts = jnp.concatenate([z.astype(jnp.int32)[None], block_owner[0]])
    grid_maps = mirror_map.reshape(2, 4, 8, length)
    half_maps = lax.dynamic_index_in_dim(grid_maps, z >> 2, 0, keepdims=False)
    maps = lax.dynamic_index_in_dim(half_maps, ket, 1, keepdims=True)
    send_map = lax.dynamic_index_in_dim(mirror_map, ((z + 4) & 7) * 8 + ket, 0, keepdims=True)

    direction = jnp.where(z >= 4, 1.0, -1.0).astype(jnp.float32)
    first = energies(vir_energy, pair_virt[0, 0])
    second = energies(vir_energy, pair_virt[0, 1])
    virtual = jnp.stack([first, second])
    chunks = ((224,), (160,))
    steps, folds, low = [], [], 0
    for pieces in chunks:
        part = own[low : low + sum(pieces)]
        low += sum(pieces)
        if steps:
            part = joined(part, steps[-1][2], pltpu.HBM)
        one = (shifted(part, -1), shifted(part, 1))
        two = (shifted(one[0], -1), shifted(one[1], 1))
        *slots, done = fold((2,), fold_facts, maps, two, pieces, ())
        three = (shifted(two[0], -1), shifted(two[1], 1))
        upper, lower = halves(*three, done if steps else fold_facts)
        far = (shifted(upper, -1), shifted(lower, 1))
        odd = (one[0], three[1], three[0], one[1])
        *slots, _ = fold((1, 3), fold_facts, maps, odd, pieces, slots)
        steps.append((part, one, three, far))
        folds.append(slots)
    fresh, low, last, sents = (), 0, (), ()
    for i, (part, one, three, far) in enumerate(steps):
        *slots, _ = fold((0,), fold_facts, maps, (part, *far), chunks[i], folds[i])
        later = steps[i + 1][1] if i + 1 < len(steps) else ()
        for piece in slots:
            piece = joined(piece, (*later, *last), pltpu.HBM)
            received = lax.all_to_all(piece, "ket", split_axis=0, concat_axis=0, tiled=True)
            ladder, sent = ladder_of(ladder_facts, send_map, all_blocks, received)
            last = (received, *sents)
            sents = (sent,)
            partner = shifted(sent, 4)
            new = update(low, own, ladder, partner, direction[None], pair_energy[:, None], virtual, fresh)
            fresh = (new,)
            low += piece.shape[2]
    return new[:, None, :]


def solution(mesh):
    placed = (
        P("pair", ("bra", "ket"), None),
        P(("bra", "ket"), "pair", None, None),
        P(("bra", "ket"), None),
        P(("bra", "ket"), None),
        P(),
        P(("bra", "ket"), None, None),
        P(),
        P("pair"),
    )
    return jax.shard_map(
        local,
        mesh=mesh,
        in_specs=placed,
        out_specs=P("pair", ("bra", "ket"), None),
        check_vma=False,
    )
```

```python
import functools

import jax
import jax.numpy as jnp
from jax import lax
from jax.experimental import pallas as pl
from jax.experimental.pallas import tpu as pltpu
from jax.sharding import PartitionSpec as P

COLS = 256
FIRST = 224
VMEM = 40 * 1024 * 1024


def one_hot(row, length, width):
    number = lax.broadcasted_iota(jnp.int32, (length, width), 0)
    return jnp.where(number == row, 1.0, 0.0).astype(jnp.bfloat16)


def fold_body(shifts, first, facts, maps, *refs):
    count = len(shifts)
    tiles = refs[: 3 if shifts == (0,) else 2 * count]
    out, done, base, other, folded, base_sem, other_sem, out_sem = refs[-8:]
    done[0] = 0
    z = facts[0]
    sign = jnp.where(z < 4, 1.0, -1.0).astype(jnp.float32)
    rows, length = folded.shape[1:]

    def fetch(i, turned):
        if shifts[i] == 0:
            cut = tiles[1].shape[0]
            return (
                pltpu.make_async_copy(tiles[0], base.at[i], base_sem.at[i]),
                pltpu.make_async_copy(tiles[1], other.at[i, pl.ds(0, cut)], other_sem.at[i, 0]),
                pltpu.make_async_copy(tiles[2], other.at[i, pl.ds(cut, cut)], other_sem.at[i, 1]),
            )
        first, second = tiles[2 * i], tiles[2 * i + 1]
        if turned:
            first, second = second, first
        return (
            pltpu.make_async_copy(first, base.at[i], base_sem.at[i]),
            pltpu.make_async_copy(second, other.at[i], other_sem.at[i, 0]),
        )

    def straight(shift):
        moved = z + shift
        return ((moved + 8) & 7) >> 2 == z >> 2

    for i, shift in enumerate(shifts):
        for turned in (False, True):

            @pl.when(straight(shift) != turned)
            def _():
                for copy in fetch(i, turned):
                    copy.start()

    for i, shift in enumerate(shifts):
        low = (z + shift + 8) & 3
        for copy in fetch(i, False):
            copy.wait()

        def column(c, carry):
            start = pl.multiple_of(c * COLS, COLS)
            picks = one_hot(maps[low, :, pl.ds(start, COLS)], length, COLS)
            turned = jnp.dot(other[i], picks, preferred_element_type=jnp.float32)
            mine = base[i, :, pl.ds(start, COLS)].astype(jnp.float32)
            folded[i, :, pl.ds(start, COLS)] = ((mine + sign * turned) * 0.5).astype(jnp.bfloat16)
            return carry

        lax.fori_loop(0, length // COLS, column, 0, unroll=True)

        for receiver in range(8):
            for half in range(2):
                segment = facts[1 + receiver * 8 + low + 4 * half]

                @pl.when(segment >= 0)
                def _():
                    start = pl.multiple_of(segment * 128, 128)
                    pltpu.make_async_copy(
                        folded.at[i, :, pl.ds(start, 128)],
                        out.at[receiver, 2 * ((shift & 3) - first) + half],
                        out_sem.at[i, receiver, half],
                    ).start()

    for i, shift in enumerate(shifts):
        low = (z + shift + 8) & 3
        for receiver in range(8):
            for half in range(2):

                @pl.when(facts[1 + receiver * 8 + low + 4 * half] >= 0)
                def _():
                    pltpu.make_async_copy(
                        folded.at[i, :, pl.ds(0, 128)],
                        out.at[receiver, 2 * ((shift & 3) - first) + half],
                        out_sem.at[i, receiver, half],
                    ).wait()


def fold(shifts, facts, maps, tiles, classes, before=(), after=()):
    rows, length = tiles[0].shape
    count = len(shifts)
    whole = pltpu.VMEM((count, rows, length), jnp.bfloat16)
    return pl.pallas_call(
        functools.partial(fold_body, shifts, classes[0]),
        in_specs=[pl.BlockSpec(memory_space=pltpu.SMEM), pl.BlockSpec(memory_space=pltpu.VMEM)]
        + [pl.BlockSpec(memory_space=pl.ANY)] * (len(tiles) + len(before) + len(after)),
        out_specs=[pl.BlockSpec(memory_space=pl.ANY), pl.BlockSpec(memory_space=pltpu.SMEM)],
        out_shape=[
            pltpu.HBM((8, 2 * len(classes), rows, 128), jnp.bfloat16),
            jax.ShapeDtypeStruct((1,), jnp.int32),
        ],
        scratch_shapes=[
            whole,
            whole,
            whole,
            pltpu.SemaphoreType.DMA((count,)),
            pltpu.SemaphoreType.DMA((count, 2)),
            pltpu.SemaphoreType.DMA((count, 8, 2)),
        ],
        compiler_params=pltpu.CompilerParams(vmem_limit_bytes=VMEM),
        cost_estimate=pl.CostEstimate(
            flops=2 * count * rows * length * length,
            bytes_accessed=count * rows * (4 * length + 16 * 256),
            transcendentals=0,
        ),
        input_output_aliases={2 + len(tiles): 0} if before else {},
        name="fold",
    )(facts, maps, *tiles, *before, *after)


def nothing(*refs):
    pass


def joined(block, others, kind=jax.ShapeDtypeStruct):
    held = pl.BlockSpec(memory_space=pl.ANY)
    return pl.pallas_call(
        nothing,
        in_specs=[held] * (1 + len(others)),
        out_specs=held,
        out_shape=kind(block.shape, block.dtype),
        input_output_aliases={0: 0},
        compiler_params=pltpu.CompilerParams(vmem_limit_bytes=VMEM),
        name="joined",
    )(block, *others)


def halves_body(first, second, _, first_out, second_out, sem):
    cut = first_out.shape[0]
    copies = (
        pltpu.make_async_copy(first.at[pl.ds(0, cut)], first_out, sem.at[0]),
        pltpu.make_async_copy(second.at[pl.ds(cut, cut)], second_out, sem.at[1]),
    )
    for copy in copies:
        copy.start()
    for copy in copies:
        copy.wait()


def halves(first, second, after):
    rows, length = first.shape
    held = pl.BlockSpec(memory_space=pl.ANY)
    part = jax.ShapeDtypeStruct((rows // 2, length), first.dtype)
    return pl.pallas_call(
        halves_body,
        in_specs=[held] * 3,
        out_specs=[held] * 2,
        out_shape=[part] * 2,
        scratch_shapes=[pltpu.SemaphoreType.DMA((2,))],
        compiler_params=pltpu.CompilerParams(vmem_limit_bytes=VMEM),
        name="halves",
    )(first, second, after)


def ladder_body(classes, facts, send_map, blocks, *refs):
    received = refs[: len(classes)]
    ladder, sent, operand, rounded, held, sem, held_sem = refs[len(classes) :]
    length = rounded.shape[1]
    parts = held_sem.shape[0]
    depth = held.shape[0] // parts

    def place(k, source=None):
        source = received[0].at[0, 0] if source is None else source
        return pltpu.make_async_copy(source, operand.at[:, pl.ds(k * 128, 128)], sem.at[k])

    def begin(k):
        tile = facts[1 + k]
        z, ket = tile >> 3, tile & 7
        away = (z - facts[0] + 8) & 3
        for held_classes, array in zip(classes, received):

            @pl.when((away >= held_classes[0]) & (away <= held_classes[-1]))
            def _():
                slot = 2 * (away - held_classes[0]) + (z >> 2)
                place(k, array.at[ket, slot]).start()

    def bring(i):
        rows = pl.ds(i * depth, depth)
        return pltpu.make_async_copy(blocks.at[rows], held.at[rows], held_sem.at[i])

    each = depth // 128
    for i in range(parts):
        for k in range(i * each, (i + 1) * each):
            begin(k)
        bring(i).start()
    for i in range(parts):
        for k in range(i * each, (i + 1) * each):
            place(k).wait()
        bring(i).wait()
        rows = slice(i * depth, (i + 1) * depth)
        for low in range(0, length, COLS):
            columns = slice(low, low + COLS)
            total = jnp.dot(operand[:, rows], held[rows, columns], preferred_element_type=jnp.float32)
            if i:
                total += ladder[:, columns]
            ladder[:, columns] = total
            if i == parts - 1:
                rounded[:, columns] = total.astype(jnp.bfloat16)
    for low in range(0, length, COLS):
        columns = slice(low, low + COLS)
        picks = one_hot(send_map[:, columns], length, COLS)
        moved = jnp.dot(rounded[...], picks, preferred_element_type=jnp.float32)
        sent[:, columns] = moved.astype(jnp.bfloat16)


def ladder_of(facts, send_map, blocks, classes, received):
    depth, length = blocks.shape
    rows = received[0].shape[2]
    vmem = pl.BlockSpec(memory_space=pltpu.VMEM)
    return pl.pallas_call(
        functools.partial(ladder_body, classes),
        in_specs=[
            pl.BlockSpec(memory_space=pltpu.SMEM),
            vmem,
        ]
        + [pl.BlockSpec(memory_space=pl.ANY)] * (1 + len(received)),
        out_specs=[vmem, vmem],
        out_shape=[
            pltpu.HBM((rows, length), jnp.float32),
            jax.ShapeDtypeStruct((rows, length), jnp.bfloat16),
        ],
        scratch_shapes=[
            pltpu.VMEM((rows, depth), jnp.bfloat16),
            pltpu.VMEM((rows, length), jnp.bfloat16),
            pltpu.VMEM((depth, length), jnp.bfloat16),
            pltpu.SemaphoreType.DMA((depth // 128,)),
            pltpu.SemaphoreType.DMA((4,)),
        ],
        compiler_params=pltpu.CompilerParams(vmem_limit_bytes=60 * 1024 * 1024),
        cost_estimate=pl.CostEstimate(
            flops=2 * rows * depth * length,
            bytes_accessed=2 * depth * (rows + length),
            transcendentals=0,
        ),
        name="ladder",
    )(facts, send_map, blocks, *received)


def update_body(low, *refs):
    own, ladder, partner, direction, occupied, virtual = refs[:6]
    out, fresh, sem = refs[-3:]
    rows = fresh.shape[0]
    step = 32
    copies = []
    for start in range(0, rows, step):
        block = slice(start, start + step)
        residual = ladder[block] + direction[0] * partner[block].astype(jnp.float32)
        denominator = occupied[block] - virtual[0:1, :] - virtual[1:2, :]
        new = own[block].astype(jnp.float32) + residual / denominator
        fresh[block] = new.astype(jnp.bfloat16)
        copies.append(
            pltpu.make_async_copy(
                fresh.at[pl.ds(start, step)], out.at[pl.ds(low + start, step)], sem.at[start // step]
            )
        )
        copies[-1].start()
    for copy in copies:
        copy.wait()


def update(low, total, own, ladder, partner, direction, occupied, virtual, before):
    rows, length = ladder.shape
    vmem, held = pl.BlockSpec(memory_space=pltpu.VMEM), pl.BlockSpec(memory_space=pl.ANY)
    return pl.pallas_call(
        functools.partial(update_body, low),
        in_specs=[vmem, vmem, vmem, pl.BlockSpec(memory_space=pltpu.SMEM), vmem, vmem]
        + [held] * len(before),
        out_specs=held,
        out_shape=pltpu.HBM((total, length), jnp.bfloat16),
        scratch_shapes=[pltpu.VMEM((rows, length), jnp.bfloat16), pltpu.SemaphoreType.DMA((rows // 32,))],
        input_output_aliases={6: 0} if before else {},
        compiler_params=pltpu.CompilerParams(vmem_limit_bytes=VMEM),
        cost_estimate=pl.CostEstimate(
            flops=8 * rows * length, bytes_accessed=10 * rows * length, transcendentals=0
        ),
        name="update",
    )(own, ladder, partner, direction, occupied, virtual, *before)


def shifted(block, by):
    return lax.ppermute(block, "bra", [(i, (i + by) % 8) for i in range(8)])


def energies(table, indices):
    number = lax.broadcasted_iota(jnp.int32, (table.shape[0], 1), 0)
    return jnp.sum(jnp.where(number == indices[None, :], table[:, None], 0.0), axis=0)


def local(
    amplitudes, integrals, screen_list, block_owner, mirror_map, pair_virt, vir_energy, pair_energy
):
    z, ket = lax.axis_index("bra"), lax.axis_index("ket")
    own = amplitudes[:, 0, :]
    rows, length = own.shape
    all_blocks = lax.all_gather(integrals[0], "pair", axis=0, tiled=True).reshape(-1, length)

    wanted = lax.all_gather(block_owner[0] * 16 + screen_list[0], "ket", axis=0)
    served = jnp.arange(8, dtype=jnp.int32) * 8 + ket
    match = (wanted >> 4)[:, None, :] == served[None, :, None]
    asked = jnp.max(jnp.where(match, wanted[:, None, :] & 15, -1), axis=2)
    fold_facts = jnp.concatenate([z.astype(jnp.int32)[None], asked.reshape(-1)])
    ladder_facts = jnp.concatenate([z.astype(jnp.int32)[None], block_owner[0]])
    grid_maps = mirror_map.reshape(2, 4, 8, length)
    half_maps = lax.dynamic_index_in_dim(grid_maps, z >> 2, 0, keepdims=False)
    maps = lax.dynamic_index_in_dim(half_maps, ket, 1, keepdims=True)
    send_map = lax.dynamic_index_in_dim(mirror_map, ((z + 4) & 7) * 8 + ket, 0, keepdims=True)

    direction = jnp.where(z >= 4, 1.0, -1.0).astype(jnp.float32)
    first = energies(vir_energy, pair_virt[0, 0])
    second = energies(vir_energy, pair_virt[0, 1])
    virtual = jnp.stack([first, second])
    cut = FIRST
    everything, later, near = (0, 1, 2, 3), (1, 2, 3), (0,)

    def climb(part, classes):
        one = (shifted(part, -1), shifted(part, 1))
        two = (shifted(one[0], -1), shifted(one[1], 1))
        slots, done = fold((2,), fold_facts, maps, two, classes)
        three = (shifted(two[0], -1), shifted(two[1], 1))
        upper, lower = halves(*three, done)
        far = (shifted(upper, -1), shifted(lower, 1))
        odd = (one[0], three[1], three[0], one[1])
        slots, _ = fold((1, 3), fold_facts, maps, odd, classes, (slots,))
        return one, far, slots

    def exchange(slots, *others):
        slots = joined(slots, others, pltpu.HBM)
        return lax.all_to_all(slots, "ket", split_axis=0, concat_axis=0, tiled=True)

    part = own[:cut]
    _, far, slots = climb(part, later)
    first_received = exchange(slots, *far)
    next_part = joined(own[cut:], far, pltpu.HBM)
    next_one, next_far, next_slots = climb(next_part, everything)
    slots, _ = fold((0,), fold_facts, maps, (part, *far), near, (), next_one)
    second_received = exchange(slots, first_received)
    next_slots, _ = fold((0,), fold_facts, maps, (next_part, *next_far), everything, (next_slots,))
    third_received = exchange(next_slots, second_received)

    work = (
        (0, part, (later, near), (first_received, second_received)),
        (cut, next_part, (everything,), (third_received,)),
    )
    before = ()
    for low, chunk, classes, received in work:
        ladder, sent = ladder_of(ladder_facts, send_map, all_blocks, classes, received)
        partner = shifted(sent, 4)
        occupied = pair_energy[low : low + chunk.shape[0], None]
        new = update(low, rows, chunk, ladder, partner, direction[None], occupied, virtual, before)
        before = (new,)
    return new[:, None, :]


def solution(mesh):
    placed = (
        P("pair", ("bra", "ket"), None),
        P(("bra", "ket"), "pair", None, None),
        P(("bra", "ket"), None),
        P(("bra", "ket"), None),
        P(),
        P(("bra", "ket"), None, None),
        P(),
        P("pair"),
    )
    return jax.shard_map(
        local,
        mesh=mesh,
        in_specs=placed,
        out_specs=P("pair", ("bra", "ket"), None),
        check_vma=False,
    )
```

```python
import functools

import jax
import jax.numpy as jnp
from jax import lax
from jax.experimental import pallas as pl
from jax.experimental.pallas import tpu as pltpu
from jax.sharding import PartitionSpec as P

COLS = 256
FIRST = 256
VMEM = 40 * 1024 * 1024


def one_hot(row, length, width):
    number = lax.broadcasted_iota(jnp.int32, (length, width), 0)
    return jnp.where(number == row, 1.0, 0.0).astype(jnp.bfloat16)


def fold_body(shifts, first, facts, maps, *refs):
    count = len(shifts)
    tiles = refs[: 3 if shifts == (0,) else 2 * count]
    out, done, base, other, folded, base_sem, other_sem, out_sem = refs[-8:]
    done[0] = 0
    z = facts[0]
    sign = jnp.where(z < 4, 1.0, -1.0).astype(jnp.float32)
    rows, length = folded.shape[1:]

    def fetch(i, turned):
        if shifts[i] == 0:
            cut = tiles[1].shape[0]
            return (
                pltpu.make_async_copy(tiles[0], base.at[i], base_sem.at[i]),
                pltpu.make_async_copy(tiles[1], other.at[i, pl.ds(0, cut)], other_sem.at[i, 0]),
                pltpu.make_async_copy(tiles[2], other.at[i, pl.ds(cut, cut)], other_sem.at[i, 1]),
            )
        first, second = tiles[2 * i], tiles[2 * i + 1]
        if turned:
            first, second = second, first
        return (
            pltpu.make_async_copy(first, base.at[i], base_sem.at[i]),
            pltpu.make_async_copy(second, other.at[i], other_sem.at[i, 0]),
        )

    def straight(shift):
        moved = z + shift
        return ((moved + 8) & 7) >> 2 == z >> 2

    for i, shift in enumerate(shifts):
        for turned in (False, True):

            @pl.when(straight(shift) != turned)
            def _():
                for copy in fetch(i, turned):
                    copy.start()

    for i, shift in enumerate(shifts):
        low = (z + shift + 8) & 3
        for copy in fetch(i, False):
            copy.wait()

        def column(c, carry):
            start = pl.multiple_of(c * COLS, COLS)
            picks = one_hot(maps[low, :, pl.ds(start, COLS)], length, COLS)
            turned = jnp.dot(other[i], picks, preferred_element_type=jnp.float32)
            mine = base[i, :, pl.ds(start, COLS)].astype(jnp.float32)
            folded[i, :, pl.ds(start, COLS)] = ((mine + sign * turned) * 0.5).astype(jnp.bfloat16)
            return carry

        lax.fori_loop(0, length // COLS, column, 0, unroll=True)

        for receiver in range(8):
            for half in range(2):
                segment = facts[1 + receiver * 8 + low + 4 * half]

                @pl.when(segment >= 0)
                def _():
                    start = pl.multiple_of(segment * 128, 128)
                    pltpu.make_async_copy(
                        folded.at[i, :, pl.ds(start, 128)],
                        out.at[receiver, 2 * ((shift & 3) - first) + half],
                        out_sem.at[i, receiver, half],
                    ).start()

    for i, shift in enumerate(shifts):
        low = (z + shift + 8) & 3
        for receiver in range(8):
            for half in range(2):

                @pl.when(facts[1 + receiver * 8 + low + 4 * half] >= 0)
                def _():
                    pltpu.make_async_copy(
                        folded.at[i, :, pl.ds(0, 128)],
                        out.at[receiver, 2 * ((shift & 3) - first) + half],
                        out_sem.at[i, receiver, half],
                    ).wait()


def fold(shifts, facts, maps, tiles, classes, before=(), after=(), weight=1):
    rows, length = tiles[0].shape
    count = len(shifts)
    whole = pltpu.VMEM((count, rows, length), jnp.bfloat16)
    return pl.pallas_call(
        functools.partial(fold_body, shifts, classes[0]),
        in_specs=[pl.BlockSpec(memory_space=pltpu.SMEM), pl.BlockSpec(memory_space=pltpu.VMEM)]
        + [pl.BlockSpec(memory_space=pl.ANY)] * (len(tiles) + len(before) + len(after)),
        out_specs=[pl.BlockSpec(memory_space=pl.ANY), pl.BlockSpec(memory_space=pltpu.SMEM)],
        out_shape=[
            pltpu.HBM((8, 2 * len(classes), rows, 128), jnp.bfloat16),
            jax.ShapeDtypeStruct((1,), jnp.int32),
        ],
        scratch_shapes=[
            whole,
            whole,
            whole,
            pltpu.SemaphoreType.DMA((count,)),
            pltpu.SemaphoreType.DMA((count, 2)),
            pltpu.SemaphoreType.DMA((count, 8, 2)),
        ],
        compiler_params=pltpu.CompilerParams(vmem_limit_bytes=VMEM),
        cost_estimate=pl.CostEstimate(
            flops=weight * 2 * count * rows * length * length,
            bytes_accessed=count * rows * (4 * length + 16 * 256),
            transcendentals=0,
        ),
        input_output_aliases={2 + len(tiles): 0} if before else {},
        name="fold",
    )(facts, maps, *tiles, *before, *after)


def nothing(*refs):
    pass


def joined(block, others, kind=jax.ShapeDtypeStruct):
    held = pl.BlockSpec(memory_space=pl.ANY)
    return pl.pallas_call(
        nothing,
        in_specs=[held] * (1 + len(others)),
        out_specs=held,
        out_shape=kind(block.shape, block.dtype),
        input_output_aliases={0: 0},
        compiler_params=pltpu.CompilerParams(vmem_limit_bytes=VMEM),
        name="joined",
    )(block, *others)


def halves_body(first, second, _, first_out, second_out, sem):
    cut = first_out.shape[0]
    copies = (
        pltpu.make_async_copy(first.at[pl.ds(0, cut)], first_out, sem.at[0]),
        pltpu.make_async_copy(second.at[pl.ds(cut, cut)], second_out, sem.at[1]),
    )
    for copy in copies:
        copy.start()
    for copy in copies:
        copy.wait()


def halves(first, second, after):
    rows, length = first.shape
    held = pl.BlockSpec(memory_space=pl.ANY)
    part = jax.ShapeDtypeStruct((rows // 2, length), first.dtype)
    return pl.pallas_call(
        halves_body,
        in_specs=[held] * 3,
        out_specs=[held] * 2,
        out_shape=[part] * 2,
        scratch_shapes=[pltpu.SemaphoreType.DMA((2,))],
        compiler_params=pltpu.CompilerParams(vmem_limit_bytes=VMEM),
        name="halves",
    )(first, second, after)


def ladder_body(classes, facts, send_map, blocks, *refs):
    received = refs[: len(classes)]
    ladder, sent, operand, rounded, held, sem, held_sem = refs[len(classes) :]
    length = rounded.shape[1]
    parts = held_sem.shape[0]
    depth = held.shape[0] // parts

    def place(k, source=None):
        source = received[0].at[0, 0] if source is None else source
        return pltpu.make_async_copy(source, operand.at[:, pl.ds(k * 128, 128)], sem.at[k])

    def begin(k):
        tile = facts[1 + k]
        z, ket = tile >> 3, tile & 7
        away = (z - facts[0] + 8) & 3
        for held_classes, array in zip(classes, received):

            @pl.when((away >= held_classes[0]) & (away <= held_classes[-1]))
            def _():
                slot = 2 * (away - held_classes[0]) + (z >> 2)
                place(k, array.at[ket, slot]).start()

    def bring(i):
        rows = pl.ds(i * depth, depth)
        return pltpu.make_async_copy(blocks.at[rows], held.at[rows], held_sem.at[i])

    each = depth // 128
    for i in range(parts):
        for k in range(i * each, (i + 1) * each):
            begin(k)
        bring(i).start()
    for i in range(parts):
        for k in range(i * each, (i + 1) * each):
            place(k).wait()
        bring(i).wait()
        rows = slice(i * depth, (i + 1) * depth)
        for low in range(0, length, COLS):
            columns = slice(low, low + COLS)
            total = jnp.dot(operand[:, rows], held[rows, columns], preferred_element_type=jnp.float32)
            if i:
                total += ladder[:, columns]
            ladder[:, columns] = total
            if i == parts - 1:
                rounded[:, columns] = total.astype(jnp.bfloat16)
    for low in range(0, length, COLS):
        columns = slice(low, low + COLS)
        picks = one_hot(send_map[:, columns], length, COLS)
        moved = jnp.dot(rounded[...], picks, preferred_element_type=jnp.float32)
        sent[:, columns] = moved.astype(jnp.bfloat16)


def ladder_of(facts, send_map, blocks, classes, received):
    depth, length = blocks.shape
    rows = received[0].shape[2]
    vmem = pl.BlockSpec(memory_space=pltpu.VMEM)
    return pl.pallas_call(
        functools.partial(ladder_body, classes),
        in_specs=[
            pl.BlockSpec(memory_space=pltpu.SMEM),
            vmem,
        ]
        + [pl.BlockSpec(memory_space=pl.ANY)] * (1 + len(received)),
        out_specs=[vmem, vmem],
        out_shape=[
            pltpu.HBM((rows, length), jnp.float32),
            jax.ShapeDtypeStruct((rows, length), jnp.bfloat16),
        ],
        scratch_shapes=[
            pltpu.VMEM((rows, depth), jnp.bfloat16),
            pltpu.VMEM((rows, length), jnp.bfloat16),
            pltpu.VMEM((depth, length), jnp.bfloat16),
            pltpu.SemaphoreType.DMA((depth // 128,)),
            pltpu.SemaphoreType.DMA((4,)),
        ],
        compiler_params=pltpu.CompilerParams(vmem_limit_bytes=60 * 1024 * 1024),
        cost_estimate=pl.CostEstimate(
            flops=2 * rows * depth * length,
            bytes_accessed=2 * depth * (rows + length),
            transcendentals=0,
        ),
        name="ladder",
    )(facts, send_map, blocks, *received)


def update_body(low, *refs):
    own, ladder, partner, direction, occupied, virtual = refs[:6]
    out, fresh, sem = refs[-3:]
    rows = fresh.shape[0]
    step = 32
    copies = []
    for start in range(0, rows, step):
        block = slice(start, start + step)
        residual = ladder[block] + direction[0] * partner[block].astype(jnp.float32)
        denominator = occupied[block] - virtual[0:1, :] - virtual[1:2, :]
        new = own[block].astype(jnp.float32) + residual / denominator
        fresh[block] = new.astype(jnp.bfloat16)
        copies.append(
            pltpu.make_async_copy(
                fresh.at[pl.ds(start, step)], out.at[pl.ds(low + start, step)], sem.at[start // step]
            )
        )
        copies[-1].start()
    for copy in copies:
        copy.wait()


def update(low, total, own, ladder, partner, direction, occupied, virtual, before):
    rows, length = ladder.shape
    vmem, held = pl.BlockSpec(memory_space=pltpu.VMEM), pl.BlockSpec(memory_space=pl.ANY)
    return pl.pallas_call(
        functools.partial(update_body, low),
        in_specs=[vmem, vmem, vmem, pl.BlockSpec(memory_space=pltpu.SMEM), vmem, vmem]
        + [held] * len(before),
        out_specs=held,
        out_shape=pltpu.HBM((total, length), jnp.bfloat16),
        scratch_shapes=[pltpu.VMEM((rows, length), jnp.bfloat16), pltpu.SemaphoreType.DMA((rows // 32,))],
        input_output_aliases={6: 0} if before else {},
        compiler_params=pltpu.CompilerParams(vmem_limit_bytes=VMEM),
        cost_estimate=pl.CostEstimate(
            flops=8 * rows * length, bytes_accessed=10 * rows * length, transcendentals=0
        ),
        name="update",
    )(own, ladder, partner, direction, occupied, virtual, *before)


def shifted(block, by):
    return lax.ppermute(block, "bra", [(i, (i + by) % 8) for i in range(8)])


def energies(table, indices):
    number = lax.broadcasted_iota(jnp.int32, (table.shape[0], 1), 0)
    return jnp.sum(jnp.where(number == indices[None, :], table[:, None], 0.0), axis=0)


def local(
    amplitudes, integrals, screen_list, block_owner, mirror_map, pair_virt, vir_energy, pair_energy
):
    z, ket = lax.axis_index("bra"), lax.axis_index("ket")
    own = amplitudes[:, 0, :]
    rows, length = own.shape
    all_blocks = lax.all_gather(integrals[0], "pair", axis=0, tiled=True).reshape(-1, length)

    wanted = lax.all_gather(block_owner[0] * 16 + screen_list[0], "ket", axis=0)
    served = jnp.arange(8, dtype=jnp.int32) * 8 + ket
    match = (wanted >> 4)[:, None, :] == served[None, :, None]
    asked = jnp.max(jnp.where(match, wanted[:, None, :] & 15, -1), axis=2)
    fold_facts = jnp.concatenate([z.astype(jnp.int32)[None], asked.reshape(-1)])
    ladder_facts = jnp.concatenate([z.astype(jnp.int32)[None], block_owner[0]])
    grid_maps = mirror_map.reshape(2, 4, 8, length)
    half_maps = lax.dynamic_index_in_dim(grid_maps, z >> 2, 0, keepdims=False)
    maps = lax.dynamic_index_in_dim(half_maps, ket, 1, keepdims=True)
    send_map = lax.dynamic_index_in_dim(mirror_map, ((z + 4) & 7) * 8 + ket, 0, keepdims=True)

    direction = jnp.where(z >= 4, 1.0, -1.0).astype(jnp.float32)
    first = energies(vir_energy, pair_virt[0, 0])
    second = energies(vir_energy, pair_virt[0, 1])
    virtual = jnp.stack([first, second])
    cut = FIRST
    everything, later, near = (0, 1, 2, 3), (1, 2, 3), (0,)

    def climb(part, classes, weight):
        one = (shifted(part, -1), shifted(part, 1))
        two = (shifted(one[0], -1), shifted(one[1], 1))
        slots, done = fold((2,), fold_facts, maps, two, classes, weight=weight)
        three = (shifted(two[0], -1), shifted(two[1], 1))
        upper, lower = halves(*three, done)
        far = (shifted(upper, -1), shifted(lower, 1))
        odd = (one[0], three[1], three[0], one[1])
        slots, _ = fold((1, 3), fold_facts, maps, odd, classes, (slots,), weight=weight)
        return one, three, far, slots

    def exchange(slots, *others):
        if others:
            slots = joined(slots, others, pltpu.HBM)
        return lax.all_to_all(slots, "ket", split_axis=0, concat_axis=0, tiled=True)

    part = own[:cut]
    _, three, far, slots = climb(part, later, 1)
    first_received = exchange(slots)
    next_part = joined(own[cut:], three, pltpu.HBM)
    next_one, _, next_far, next_slots = climb(next_part, everything, 8)
    slots, _ = fold((0,), fold_facts, maps, (part, *far), near, (), next_one)
    second_received = exchange(slots, first_received)
    next_slots, _ = fold((0,), fold_facts, maps, (next_part, *next_far), everything, (next_slots,), weight=8)
    third_received = exchange(next_slots, second_received)

    work = (
        (0, part, (later, near), (first_received, second_received)),
        (cut, next_part, (everything,), (third_received,)),
    )
    before = ()
    for low, chunk, classes, received in work:
        ladder, sent = ladder_of(ladder_facts, send_map, all_blocks, classes, received)
        partner = shifted(sent, 4)
        occupied = pair_energy[low : low + chunk.shape[0], None]
        new = update(low, rows, chunk, ladder, partner, direction[None], occupied, virtual, before)
        before = (new,)
    return new[:, None, :]


def solution(mesh):
    placed = (
        P("pair", ("bra", "ket"), None),
        P(("bra", "ket"), "pair", None, None),
        P(("bra", "ket"), None),
        P(("bra", "ket"), None),
        P(),
        P(("bra", "ket"), None, None),
        P(),
        P("pair"),
    )
    return jax.shard_map(
        local,
        mesh=mesh,
        in_specs=placed,
        out_specs=P("pair", ("bra", "ket"), None),
        check_vma=False,
    )
```

```python
import functools

import jax
import jax.numpy as jnp
from jax import lax
from jax.experimental import pallas as pl
from jax.experimental.pallas import tpu as pltpu
from jax.sharding import PartitionSpec as P

COLS = 256
WEIGHT = 1
VMEM = 40 * 1024 * 1024


def one_hot(row, length, width):
    number = lax.broadcasted_iota(jnp.int32, (length, width), 0)
    return jnp.where(number == row, 1.0, 0.0).astype(jnp.bfloat16)


def fold_body(shifts, pieces, facts, maps, *refs):
    count = len(shifts)
    tiles = refs[: 3 if shifts == (0,) else 2 * count]
    done, base, other, folded, base_sem, other_sem, out_sem = refs[-7:]
    outs = refs[-7 - len(pieces) : -7]
    done[0] = 0
    z = facts[0]
    sign = jnp.where(z < 4, 1.0, -1.0).astype(jnp.float32)
    rows, length = folded.shape[1:]

    def fetch(i, turned):
        if shifts[i] == 0:
            cut = tiles[1].shape[0]
            return (
                pltpu.make_async_copy(tiles[0], base.at[i], base_sem.at[i]),
                pltpu.make_async_copy(tiles[1], other.at[i, pl.ds(0, cut)], other_sem.at[i, 0]),
                pltpu.make_async_copy(tiles[2], other.at[i, pl.ds(cut, cut)], other_sem.at[i, 1]),
            )
        first, second = tiles[2 * i], tiles[2 * i + 1]
        if turned:
            first, second = second, first
        return (
            pltpu.make_async_copy(first, base.at[i], base_sem.at[i]),
            pltpu.make_async_copy(second, other.at[i], other_sem.at[i, 0]),
        )

    def straight(shift):
        moved = z + shift
        return ((moved + 8) & 7) >> 2 == z >> 2

    for i, shift in enumerate(shifts):
        for turned in (False, True):

            @pl.when(straight(shift) != turned)
            def _():
                for copy in fetch(i, turned):
                    copy.start()

    sends = []
    for i, shift in enumerate(shifts):
        low = (z + shift + 8) & 3
        for copy in fetch(i, False):
            copy.wait()

        def column(c, carry):
            start = pl.multiple_of(c * COLS, COLS)
            picks = one_hot(maps[low, :, pl.ds(start, COLS)], length, COLS)
            turned = jnp.dot(other[i], picks, preferred_element_type=jnp.float32)
            mine = base[i, :, pl.ds(start, COLS)].astype(jnp.float32)
            folded[i, :, pl.ds(start, COLS)] = ((mine + sign * turned) * 0.5).astype(jnp.bfloat16)
            return carry

        lax.fori_loop(0, length // COLS, column, 0, unroll=True)

        def send(receiver, half, start, i=i, shift=shift):
            copies, low = [], 0
            for p, (out, count) in enumerate(zip(outs, pieces)):
                source = folded.at[i, pl.ds(low, count), pl.ds(start, 128)]
                place = out.at[receiver, 2 * (shift & 3) + half]
                copies.append(
                    pltpu.make_async_copy(source, place, out_sem.at[i, receiver, 2 * p + half])
                )
                low += count
            return copies

        sends.append(send)
        for receiver in range(8):
            for half in range(2):
                segment = facts[1 + receiver * 8 + low + 4 * half]

                @pl.when(segment >= 0)
                def _():
                    for copy in send(receiver, half, pl.multiple_of(segment * 128, 128)):
                        copy.start()

    for i, shift in enumerate(shifts):
        low = (z + shift + 8) & 3
        for receiver in range(8):
            for half in range(2):

                @pl.when(facts[1 + receiver * 8 + low + 4 * half] >= 0)
                def _():
                    for copy in sends[i](receiver, half, 0):
                        copy.wait()


def fold(shifts, facts, maps, tiles, pieces, before, weight):
    rows, length = tiles[0].shape
    count = len(shifts)
    whole = pltpu.VMEM((count, rows, length), jnp.bfloat16)
    return pl.pallas_call(
        functools.partial(fold_body, shifts, pieces),
        in_specs=[pl.BlockSpec(memory_space=pltpu.SMEM), pl.BlockSpec(memory_space=pltpu.VMEM)]
        + [pl.BlockSpec(memory_space=pl.ANY)] * (len(tiles) + len(before)),
        out_specs=[pl.BlockSpec(memory_space=pl.ANY)] * len(pieces)
        + [pl.BlockSpec(memory_space=pltpu.SMEM)],
        out_shape=[pltpu.HBM((8, 8, piece, 128), jnp.bfloat16) for piece in pieces]
        + [jax.ShapeDtypeStruct((1,), jnp.int32)],
        scratch_shapes=[
            whole,
            whole,
            whole,
            pltpu.SemaphoreType.DMA((count,)),
            pltpu.SemaphoreType.DMA((count, 2)),
            pltpu.SemaphoreType.DMA((count, 8, 2 * len(pieces))),
        ],
        compiler_params=pltpu.CompilerParams(vmem_limit_bytes=VMEM),
        cost_estimate=pl.CostEstimate(
            flops=weight * 2 * count * rows * length * length,
            bytes_accessed=count * rows * (4 * length + 16 * 256),
            transcendentals=0,
        ),
        input_output_aliases={2 + len(tiles) + p: p for p in range(len(before))},
        name="fold",
    )(facts, maps, *tiles, *before)


def nothing(*refs):
    pass


def joined(block, others, kind=jax.ShapeDtypeStruct):
    held = pl.BlockSpec(memory_space=pl.ANY)
    return pl.pallas_call(
        nothing,
        in_specs=[held] * (1 + len(others)),
        out_specs=held,
        out_shape=kind(block.shape, block.dtype),
        input_output_aliases={0: 0},
        compiler_params=pltpu.CompilerParams(vmem_limit_bytes=VMEM),
        name="joined",
    )(block, *others)


def halves_body(first, second, _, first_out, second_out, sem):
    cut = first_out.shape[0]
    copies = (
        pltpu.make_async_copy(first.at[pl.ds(0, cut)], first_out, sem.at[0]),
        pltpu.make_async_copy(second.at[pl.ds(cut, cut)], second_out, sem.at[1]),
    )
    for copy in copies:
        copy.start()
    for copy in copies:
        copy.wait()


def halves(first, second, after):
    rows, length = first.shape
    held = pl.BlockSpec(memory_space=pl.ANY)
    part = jax.ShapeDtypeStruct((rows // 2, length), first.dtype)
    return pl.pallas_call(
        halves_body,
        in_specs=[held] * 3,
        out_specs=[held] * 2,
        out_shape=[part] * 2,
        scratch_shapes=[pltpu.SemaphoreType.DMA((2,))],
        compiler_params=pltpu.CompilerParams(vmem_limit_bytes=VMEM),
        name="halves",
    )(first, second, after)


def ladder_body(facts, maps, blocks, received, ladder, sent, operand, rounded, held, sem, held_sem):
    length = rounded.shape[1]
    parts = held_sem.shape[0]
    depth = held.shape[0] // parts

    def place(k):
        tile = facts[65 + k]
        z, ket = tile >> 3, tile & 7
        slot = 2 * ((z - facts[0] + 8) & 3) + (z >> 2)
        where = operand.at[:, pl.ds(k * 128, 128)]
        return pltpu.make_async_copy(received.at[ket, slot], where, sem.at[k])

    def bring(i):
        rows = pl.ds(i * depth, depth)
        return pltpu.make_async_copy(blocks.at[rows], held.at[rows], held_sem.at[i])

    each = depth // 128
    for i in range(parts):
        for k in range(i * each, (i + 1) * each):
            place(k).start()
        bring(i).start()
    for i in range(parts):
        for k in range(i * each, (i + 1) * each):
            place(k).wait()
        bring(i).wait()
        rows = slice(i * depth, (i + 1) * depth)
        for low in range(0, length, COLS):
            columns = slice(low, low + COLS)
            total = jnp.dot(operand[:, rows], held[rows, columns], preferred_element_type=jnp.float32)
            if i:
                total += ladder[:, columns]
            ladder[:, columns] = total
            if i == parts - 1:
                rounded[:, columns] = total.astype(jnp.bfloat16)
    for low in range(0, length, COLS):
        columns = slice(low, low + COLS)
        picks = one_hot(maps[4, :, columns], length, COLS)
        moved = jnp.dot(rounded[...], picks, preferred_element_type=jnp.float32)
        sent[:, columns] = moved.astype(jnp.bfloat16)


def ladder_of(facts, maps, blocks, received):
    depth, length = blocks.shape
    rows = received.shape[2]
    vmem = pl.BlockSpec(memory_space=pltpu.VMEM)
    return pl.pallas_call(
        ladder_body,
        in_specs=[
            pl.BlockSpec(memory_space=pltpu.SMEM),
            vmem,
            pl.BlockSpec(memory_space=pl.ANY),
            pl.BlockSpec(memory_space=pl.ANY),
        ],
        out_specs=[vmem, vmem],
        out_shape=[
            pltpu.HBM((rows, length), jnp.float32),
            jax.ShapeDtypeStruct((rows, length), jnp.bfloat16),
        ],
        scratch_shapes=[
            pltpu.VMEM((rows, depth), jnp.bfloat16),
            pltpu.VMEM((rows, length), jnp.bfloat16),
            pltpu.VMEM((depth, length), jnp.bfloat16),
            pltpu.SemaphoreType.DMA((depth // 128,)),
            pltpu.SemaphoreType.DMA((4,)),
        ],
        compiler_params=pltpu.CompilerParams(vmem_limit_bytes=60 * 1024 * 1024),
        cost_estimate=pl.CostEstimate(
            flops=2 * rows * depth * length,
            bytes_accessed=2 * depth * (rows + length),
            transcendentals=0,
        ),
        name="ladder",
    )(facts, maps, blocks, received)


def update_body(low, *refs):
    own, ladder, partner, direction, occupied, virtual = refs[:6]
    out, fresh, sem = refs[-3:]
    rows = fresh.shape[0]
    step = 32
    copies = []
    for start in range(0, rows, step):
        block = slice(start, start + step)
        residual = ladder[block] + direction[0] * partner[block].astype(jnp.float32)
        denominator = occupied[block] - virtual[0:1, :] - virtual[1:2, :]
        new = own[block].astype(jnp.float32) + residual / denominator
        fresh[block] = new.astype(jnp.bfloat16)
        copies.append(
            pltpu.make_async_copy(
                fresh.at[pl.ds(start, step)], out.at[pl.ds(low + start, step)], sem.at[start // step]
            )
        )
        copies[-1].start()
    for copy in copies:
        copy.wait()


def update(low, total, own, ladder, partner, direction, occupied, virtual, before):
    rows, length = ladder.shape
    vmem, held = pl.BlockSpec(memory_space=pltpu.VMEM), pl.BlockSpec(memory_space=pl.ANY)
    return pl.pallas_call(
        functools.partial(update_body, low),
        in_specs=[vmem, vmem, vmem, pl.BlockSpec(memory_space=pltpu.SMEM), vmem, vmem]
        + [held] * len(before),
        out_specs=held,
        out_shape=pltpu.HBM((total, length), jnp.bfloat16),
        scratch_shapes=[pltpu.VMEM((rows, length), jnp.bfloat16), pltpu.SemaphoreType.DMA((rows // 32,))],
        input_output_aliases={6: 0} if before else {},
        compiler_params=pltpu.CompilerParams(vmem_limit_bytes=VMEM),
        cost_estimate=pl.CostEstimate(
            flops=8 * rows * length, bytes_accessed=10 * rows * length, transcendentals=0
        ),
        name="update",
    )(own, ladder, partner, direction, occupied, virtual, *before)


def shifted(block, by):
    return lax.ppermute(block, "bra", [(i, (i + by) % 8) for i in range(8)])


def energies(table, indices):
    number = lax.broadcasted_iota(jnp.int32, (table.shape[0], 1), 0)
    return jnp.sum(jnp.where(number == indices[None, :], table[:, None], 0.0), axis=0)


def local(
    amplitudes, integrals, screen_list, block_owner, mirror_map, pair_virt, vir_energy, pair_energy
):
    z, ket = lax.axis_index("bra"), lax.axis_index("ket")
    own = amplitudes[:, 0, :]
    rows, length = own.shape
    all_blocks = lax.all_gather(integrals[0], "pair", axis=0, tiled=True).reshape(-1, length)

    wanted = lax.all_gather(block_owner[0] * 16 + screen_list[0], "ket", axis=0)
    served = jnp.arange(8, dtype=jnp.int32) * 8 + ket
    match = (wanted >> 4)[:, None, :] == served[None, :, None]
    asked = jnp.max(jnp.where(match, wanted[:, None, :] & 15, -1), axis=2)
    facts = jnp.concatenate([z.astype(jnp.int32)[None], asked.reshape(-1), block_owner[0]])
    grid_maps = mirror_map.reshape(2, 4, 8, length)
    half_maps = lax.dynamic_index_in_dim(grid_maps, z >> 2, 0, keepdims=False)
    maps = lax.dynamic_index_in_dim(half_maps, ket, 1, keepdims=True)
    send_map = lax.dynamic_index_in_dim(mirror_map, ((z + 4) & 7) * 8 + ket, 0, keepdims=True)
    maps = jnp.concatenate([maps, send_map[None]])

    direction = jnp.where(z >= 4, 1.0, -1.0).astype(jnp.float32)
    first = energies(vir_energy, pair_virt[0, 0])
    second = energies(vir_energy, pair_virt[0, 1])
    virtual = jnp.stack([first, second])
    chunks = ((224,), (160,))
    steps, folds, low = [], [], 0
    for pieces in chunks:
        part = own[low : low + sum(pieces)]
        low += sum(pieces)
        if steps:
            part = joined(part, steps[-1][2], pltpu.HBM)
        one = (shifted(part, -1), shifted(part, 1))
        two = (shifted(one[0], -1), shifted(one[1], 1))
        weight = WEIGHT if steps else 1
        *slots, done = fold((2,), facts, maps, two, pieces, (), weight)
        three = (shifted(two[0], -1), shifted(two[1], 1))
        upper, lower = halves(*three, done if steps else facts)
        far = (shifted(upper, -1), shifted(lower, 1))
        odd = (one[0], three[1], three[0], one[1])
        *slots, _ = fold((1, 3), facts, maps, odd, pieces, slots, weight)
        steps.append((part, one, three, far))
        folds.append(slots)
    fresh, low, last = (), 0, ()
    for i, (part, one, three, far) in enumerate(steps):
        weight = WEIGHT if i else 1
        *slots, _ = fold((0,), facts, maps, (part, *far), chunks[i], folds[i], weight)
        for piece in slots:
            later = steps[i + 1][1] if i + 1 < len(steps) else ()
            piece = joined(piece, (*later, *last), pltpu.HBM)
            received = lax.all_to_all(piece, "ket", split_axis=0, concat_axis=0, tiled=True)
            ladder, sent = ladder_of(facts, maps, all_blocks, received)
            last = (received,)
            partner = shifted(sent, 4)
            chunk = own[low : low + piece.shape[2]]
            occupied = pair_energy[low : low + piece.shape[2], None]
            new = update(
                low, rows, chunk, ladder, partner, direction[None], occupied, virtual, fresh
            )
            fresh = (new,)
            low += piece.shape[2]
    return new[:, None, :]


def solution(mesh):
    placed = (
        P("pair", ("bra", "ket"), None),
        P(("bra", "ket"), "pair", None, None),
        P(("bra", "ket"), None),
        P(("bra", "ket"), None),
        P(),
        P(("bra", "ket"), None, None),
        P(),
        P("pair"),
    )
    return jax.shard_map(
        local,
        mesh=mesh,
        in_specs=placed,
        out_specs=P("pair", ("bra", "ket"), None),
        check_vma=False,
    )
```

```python
import functools

import jax
import jax.numpy as jnp
from jax import lax
from jax.experimental import pallas as pl
from jax.experimental.pallas import tpu as pltpu
from jax.sharding import PartitionSpec as P

COLS = 256
WEIGHT = 1
VMEM = 40 * 1024 * 1024


def one_hot(row, length, width):
    number = lax.broadcasted_iota(jnp.int32, (length, width), 0)
    return jnp.where(number == row, 1.0, 0.0).astype(jnp.bfloat16)


def fold_body(shifts, pieces, facts, maps, *refs):
    count = len(shifts)
    tiles = refs[: 3 if shifts == (0,) else 2 * count]
    done, base, other, folded, base_sem, other_sem, out_sem = refs[-7:]
    outs = refs[-7 - len(pieces) : -7]
    done[0] = 0
    z = facts[0]
    sign = jnp.where(z < 4, 1.0, -1.0).astype(jnp.float32)
    rows, length = folded.shape[1:]

    def fetch(i, turned):
        if shifts[i] == 0:
            cut = tiles[1].shape[0]
            return (
                pltpu.make_async_copy(tiles[0], base.at[i], base_sem.at[i]),
                pltpu.make_async_copy(tiles[1], other.at[i, pl.ds(0, cut)], other_sem.at[i, 0]),
                pltpu.make_async_copy(tiles[2], other.at[i, pl.ds(cut, cut)], other_sem.at[i, 1]),
            )
        first, second = tiles[2 * i], tiles[2 * i + 1]
        if turned:
            first, second = second, first
        return (
            pltpu.make_async_copy(first, base.at[i], base_sem.at[i]),
            pltpu.make_async_copy(second, other.at[i], other_sem.at[i, 0]),
        )

    def straight(shift):
        moved = z + shift
        return ((moved + 8) & 7) >> 2 == z >> 2

    for i, shift in enumerate(shifts):
        for turned in (False, True):

            @pl.when(straight(shift) != turned)
            def _():
                for copy in fetch(i, turned):
                    copy.start()

    sends = []
    for i, shift in enumerate(shifts):
        low = (z + shift + 8) & 3
        for copy in fetch(i, False):
            copy.wait()

        def column(c, carry):
            start = pl.multiple_of(c * COLS, COLS)
            picks = one_hot(maps[low, :, pl.ds(start, COLS)], length, COLS)
            turned = jnp.dot(other[i], picks, preferred_element_type=jnp.float32)
            mine = base[i, :, pl.ds(start, COLS)].astype(jnp.float32)
            folded[i, :, pl.ds(start, COLS)] = ((mine + sign * turned) * 0.5).astype(jnp.bfloat16)
            return carry

        lax.fori_loop(0, length // COLS, column, 0, unroll=True)

        def send(receiver, half, start, i=i, shift=shift):
            copies, low = [], 0
            for p, (out, count) in enumerate(zip(outs, pieces)):
                source = folded.at[i, pl.ds(low, count), pl.ds(start, 128)]
                place = out.at[receiver, 2 * (shift & 3) + half]
                copies.append(
                    pltpu.make_async_copy(source, place, out_sem.at[i, receiver, 2 * p + half])
                )
                low += count
            return copies

        sends.append(send)
        for receiver in range(8):
            for half in range(2):
                segment = facts[1 + receiver * 8 + low + 4 * half]

                @pl.when(segment >= 0)
                def _():
                    for copy in send(receiver, half, pl.multiple_of(segment * 128, 128)):
                        copy.start()

    for i, shift in enumerate(shifts):
        low = (z + shift + 8) & 3
        for receiver in range(8):
            for half in range(2):

                @pl.when(facts[1 + receiver * 8 + low + 4 * half] >= 0)
                def _():
                    for copy in sends[i](receiver, half, 0):
                        copy.wait()


def fold(shifts, facts, maps, tiles, pieces, before, weight):
    rows, length = tiles[0].shape
    count = len(shifts)
    whole = pltpu.VMEM((count, rows, length), jnp.bfloat16)
    return pl.pallas_call(
        functools.partial(fold_body, shifts, pieces),
        in_specs=[pl.BlockSpec(memory_space=pltpu.SMEM), pl.BlockSpec(memory_space=pltpu.VMEM)]
        + [pl.BlockSpec(memory_space=pl.ANY)] * (len(tiles) + len(before)),
        out_specs=[pl.BlockSpec(memory_space=pl.ANY)] * len(pieces)
        + [pl.BlockSpec(memory_space=pltpu.SMEM)],
        out_shape=[pltpu.HBM((8, 8, piece, 128), jnp.bfloat16) for piece in pieces]
        + [jax.ShapeDtypeStruct((1,), jnp.int32)],
        scratch_shapes=[
            whole,
            whole,
            whole,
            pltpu.SemaphoreType.DMA((count,)),
            pltpu.SemaphoreType.DMA((count, 2)),
            pltpu.SemaphoreType.DMA((count, 8, 2 * len(pieces))),
        ],
        compiler_params=pltpu.CompilerParams(vmem_limit_bytes=VMEM),
        cost_estimate=pl.CostEstimate(
            flops=weight * 2 * count * rows * length * length,
            bytes_accessed=count * rows * (4 * length + 16 * 256),
            transcendentals=0,
        ),
        input_output_aliases={2 + len(tiles) + p: p for p in range(len(before))},
        name="fold",
    )(facts, maps, *tiles, *before)


def nothing(*refs):
    pass


def joined(block, others, kind=jax.ShapeDtypeStruct):
    held = pl.BlockSpec(memory_space=pl.ANY)
    return pl.pallas_call(
        nothing,
        in_specs=[held] * (1 + len(others)),
        out_specs=held,
        out_shape=kind(block.shape, block.dtype),
        input_output_aliases={0: 0},
        compiler_params=pltpu.CompilerParams(vmem_limit_bytes=VMEM),
        name="joined",
    )(block, *others)


def halves_body(first, second, _, first_out, second_out, sem):
    cut = first_out.shape[0]
    copies = (
        pltpu.make_async_copy(first.at[pl.ds(0, cut)], first_out, sem.at[0]),
        pltpu.make_async_copy(second.at[pl.ds(cut, cut)], second_out, sem.at[1]),
    )
    for copy in copies:
        copy.start()
    for copy in copies:
        copy.wait()


def halves(first, second, after):
    rows, length = first.shape
    held = pl.BlockSpec(memory_space=pl.ANY)
    part = jax.ShapeDtypeStruct((rows // 2, length), first.dtype)
    return pl.pallas_call(
        halves_body,
        in_specs=[held] * 3,
        out_specs=[held] * 2,
        out_shape=[part] * 2,
        scratch_shapes=[pltpu.SemaphoreType.DMA((2,))],
        compiler_params=pltpu.CompilerParams(vmem_limit_bytes=VMEM),
        name="halves",
    )(first, second, after)


def ladder_body(facts, maps, blocks, received, ladder, sent, operand, rounded, held, sem, held_sem):
    length = rounded.shape[1]
    parts = held_sem.shape[0]
    depth = held.shape[0] // parts

    def place(k):
        tile = facts[65 + k]
        z, ket = tile >> 3, tile & 7
        slot = 2 * ((z - facts[0] + 8) & 3) + (z >> 2)
        where = operand.at[:, pl.ds(k * 128, 128)]
        return pltpu.make_async_copy(received.at[ket, slot], where, sem.at[k])

    def bring(i):
        rows = pl.ds(i * depth, depth)
        return pltpu.make_async_copy(blocks.at[rows], held.at[rows], held_sem.at[i])

    each = depth // 128
    for i in range(parts):
        for k in range(i * each, (i + 1) * each):
            place(k).start()
        bring(i).start()
    for i in range(parts):
        for k in range(i * each, (i + 1) * each):
            place(k).wait()
        bring(i).wait()
        rows = slice(i * depth, (i + 1) * depth)
        for low in range(0, length, COLS):
            columns = slice(low, low + COLS)
            total = jnp.dot(operand[:, rows], held[rows, columns], preferred_element_type=jnp.float32)
            if i:
                total += ladder[:, columns]
            ladder[:, columns] = total
            if i == parts - 1:
                rounded[:, columns] = total.astype(jnp.bfloat16)
    for low in range(0, length, COLS):
        columns = slice(low, low + COLS)
        picks = one_hot(maps[4, :, columns], length, COLS)
        moved = jnp.dot(rounded[...], picks, preferred_element_type=jnp.float32)
        sent[:, columns] = moved.astype(jnp.bfloat16)


def ladder_of(facts, maps, blocks, received):
    depth, length = blocks.shape
    rows = received.shape[2]
    vmem = pl.BlockSpec(memory_space=pltpu.VMEM)
    return pl.pallas_call(
        ladder_body,
        in_specs=[
            pl.BlockSpec(memory_space=pltpu.SMEM),
            vmem,
            pl.BlockSpec(memory_space=pl.ANY),
            pl.BlockSpec(memory_space=pl.ANY),
        ],
        out_specs=[vmem, vmem],
        out_shape=[
            pltpu.HBM((rows, length), jnp.float32),
            jax.ShapeDtypeStruct((rows, length), jnp.bfloat16),
        ],
        scratch_shapes=[
            pltpu.VMEM((rows, depth), jnp.bfloat16),
            pltpu.VMEM((rows, length), jnp.bfloat16),
            pltpu.VMEM((depth, length), jnp.bfloat16),
            pltpu.SemaphoreType.DMA((depth // 128,)),
            pltpu.SemaphoreType.DMA((4,)),
        ],
        compiler_params=pltpu.CompilerParams(vmem_limit_bytes=60 * 1024 * 1024),
        cost_estimate=pl.CostEstimate(
            flops=2 * rows * depth * length,
            bytes_accessed=2 * depth * (rows + length),
            transcendentals=0,
        ),
        name="ladder",
    )(facts, maps, blocks, received)


def update_body(low, *refs):
    own, ladder, partner, direction, occupied, virtual = refs[:6]
    out, fresh, sem = refs[-3:]
    rows = fresh.shape[0]
    step = 32
    copies = []
    for start in range(0, rows, step):
        block = slice(start, start + step)
        residual = ladder[block] + direction[0] * partner[block].astype(jnp.float32)
        denominator = occupied[block] - virtual[0:1, :] - virtual[1:2, :]
        new = own[block].astype(jnp.float32) + residual / denominator
        fresh[block] = new.astype(jnp.bfloat16)
        copies.append(
            pltpu.make_async_copy(
                fresh.at[pl.ds(start, step)], out.at[pl.ds(low + start, step)], sem.at[start // step]
            )
        )
        copies[-1].start()
    for copy in copies:
        copy.wait()


def update(low, total, own, ladder, partner, direction, occupied, virtual, before):
    rows, length = ladder.shape
    vmem, held = pl.BlockSpec(memory_space=pltpu.VMEM), pl.BlockSpec(memory_space=pl.ANY)
    return pl.pallas_call(
        functools.partial(update_body, low),
        in_specs=[vmem, vmem, vmem, pl.BlockSpec(memory_space=pltpu.SMEM), vmem, vmem]
        + [held] * len(before),
        out_specs=held,
        out_shape=pltpu.HBM((total, length), jnp.bfloat16),
        scratch_shapes=[pltpu.VMEM((rows, length), jnp.bfloat16), pltpu.SemaphoreType.DMA((rows // 32,))],
        input_output_aliases={6: 0} if before else {},
        compiler_params=pltpu.CompilerParams(vmem_limit_bytes=VMEM),
        cost_estimate=pl.CostEstimate(
            flops=8 * rows * length, bytes_accessed=10 * rows * length, transcendentals=0
        ),
        name="update",
    )(own, ladder, partner, direction, occupied, virtual, *before)


def shifted(block, by):
    return lax.ppermute(block, "bra", [(i, (i + by) % 8) for i in range(8)])


def energies(table, indices):
    number = lax.broadcasted_iota(jnp.int32, (table.shape[0], 1), 0)
    return jnp.sum(jnp.where(number == indices[None, :], table[:, None], 0.0), axis=0)


def local(
    amplitudes, integrals, screen_list, block_owner, mirror_map, pair_virt, vir_energy, pair_energy
):
    z, ket = lax.axis_index("bra"), lax.axis_index("ket")
    own = amplitudes[:, 0, :]
    rows, length = own.shape
    all_blocks = lax.all_gather(integrals[0], "pair", axis=0, tiled=True).reshape(-1, length)

    wanted = lax.all_gather(block_owner[0] * 16 + screen_list[0], "ket", axis=0)
    served = jnp.arange(8, dtype=jnp.int32) * 8 + ket
    match = (wanted >> 4)[:, None, :] == served[None, :, None]
    asked = jnp.max(jnp.where(match, wanted[:, None, :] & 15, -1), axis=2)
    facts = jnp.concatenate([z.astype(jnp.int32)[None], asked.reshape(-1), block_owner[0]])
    grid_maps = mirror_map.reshape(2, 4, 8, length)
    half_maps = lax.dynamic_index_in_dim(grid_maps, z >> 2, 0, keepdims=False)
    maps = lax.dynamic_index_in_dim(half_maps, ket, 1, keepdims=True)
    send_map = lax.dynamic_index_in_dim(mirror_map, ((z + 4) & 7) * 8 + ket, 0, keepdims=True)
    maps = jnp.concatenate([maps, send_map[None]])

    direction = jnp.where(z >= 4, 1.0, -1.0).astype(jnp.float32)
    first = energies(vir_energy, pair_virt[0, 0])
    second = energies(vir_energy, pair_virt[0, 1])
    virtual = jnp.stack([first, second])
    chunks = ((256,), (128,))
    steps, folds, low = [], [], 0
    for pieces in chunks:
        part = own[low : low + sum(pieces)]
        low += sum(pieces)
        if steps:
            part = joined(part, steps[-1][3], pltpu.HBM)
        one = (shifted(part, -1), shifted(part, 1))
        two = (shifted(one[0], -1), shifted(one[1], 1))
        weight = WEIGHT if steps else 1
        *slots, done = fold((2,), facts, maps, two, pieces, (), weight)
        three = (shifted(two[0], -1), shifted(two[1], 1))
        upper, lower = halves(*three, done)
        far = (shifted(upper, -1), shifted(lower, 1))
        odd = (one[0], three[1], three[0], one[1])
        *slots, _ = fold((1, 3), facts, maps, odd, pieces, slots, weight)
        steps.append((part, one, three, far))
        folds.append(slots)
    fresh, low, last = (), 0, ()
    for i, (part, one, three, far) in enumerate(steps):
        weight = WEIGHT if i else 1
        *slots, _ = fold((0,), facts, maps, (part, *far), chunks[i], folds[i], weight)
        for piece in slots:
            if last:
                piece = joined(piece, last, pltpu.HBM)
            received = lax.all_to_all(piece, "ket", split_axis=0, concat_axis=0, tiled=True)
            ladder, sent = ladder_of(facts, maps, all_blocks, received)
            last = (received,)
            partner = shifted(sent, 4)
            chunk = own[low : low + piece.shape[2]]
            occupied = pair_energy[low : low + piece.shape[2], None]
            new = update(
                low, rows, chunk, ladder, partner, direction[None], occupied, virtual, fresh
            )
            fresh = (new,)
            low += piece.shape[2]
    return new[:, None, :]


def solution(mesh):
    placed = (
        P("pair", ("bra", "ket"), None),
        P(("bra", "ket"), "pair", None, None),
        P(("bra", "ket"), None),
        P(("bra", "ket"), None),
        P(),
        P(("bra", "ket"), None, None),
        P(),
        P("pair"),
    )
    return jax.shard_map(
        local,
        mesh=mesh,
        in_specs=placed,
        out_specs=P("pair", ("bra", "ket"), None),
        check_vma=False,
    )
```

```python
import functools

import jax
import jax.numpy as jnp
from jax import lax
from jax.experimental import pallas as pl
from jax.experimental.pallas import tpu as pltpu
from jax.sharding import PartitionSpec as P

COLS = 256
WEIGHT = 1
VMEM = 40 * 1024 * 1024


def one_hot(row, length, width):
    number = lax.broadcasted_iota(jnp.int32, (length, width), 0)
    return jnp.where(number == row, 1.0, 0.0).astype(jnp.bfloat16)


def fold_body(shifts, pieces, facts, maps, *refs):
    count = len(shifts)
    tiles = refs[: 3 if shifts == (0,) else 2 * count]
    done, base, other, folded, base_sem, other_sem, out_sem = refs[-7:]
    outs = refs[-7 - len(pieces) : -7]
    done[0] = 0
    z = facts[0]
    sign = jnp.where(z < 4, 1.0, -1.0).astype(jnp.float32)
    rows, length = folded.shape[1:]

    def fetch(i, turned):
        if shifts[i] == 0:
            cut = tiles[1].shape[0]
            return (
                pltpu.make_async_copy(tiles[0], base.at[i], base_sem.at[i]),
                pltpu.make_async_copy(tiles[1], other.at[i, pl.ds(0, cut)], other_sem.at[i, 0]),
                pltpu.make_async_copy(tiles[2], other.at[i, pl.ds(cut, cut)], other_sem.at[i, 1]),
            )
        first, second = tiles[2 * i], tiles[2 * i + 1]
        if turned:
            first, second = second, first
        return (
            pltpu.make_async_copy(first, base.at[i], base_sem.at[i]),
            pltpu.make_async_copy(second, other.at[i], other_sem.at[i, 0]),
        )

    def straight(shift):
        moved = z + shift
        return ((moved + 8) & 7) >> 2 == z >> 2

    for i, shift in enumerate(shifts):
        for turned in (False, True):

            @pl.when(straight(shift) != turned)
            def _():
                for copy in fetch(i, turned):
                    copy.start()

    sends = []
    for i, shift in enumerate(shifts):
        low = (z + shift + 8) & 3
        for copy in fetch(i, False):
            copy.wait()

        def column(c, carry):
            start = pl.multiple_of(c * COLS, COLS)
            picks = one_hot(maps[low, :, pl.ds(start, COLS)], length, COLS)
            turned = jnp.dot(other[i], picks, preferred_element_type=jnp.float32)
            mine = base[i, :, pl.ds(start, COLS)].astype(jnp.float32)
            folded[i, :, pl.ds(start, COLS)] = ((mine + sign * turned) * 0.5).astype(jnp.bfloat16)
            return carry

        lax.fori_loop(0, length // COLS, column, 0, unroll=True)

        def send(receiver, half, start, i=i, shift=shift):
            copies, low = [], 0
            for p, (out, count) in enumerate(zip(outs, pieces)):
                source = folded.at[i, pl.ds(low, count), pl.ds(start, 128)]
                place = out.at[receiver, 2 * (shift & 3) + half]
                copies.append(
                    pltpu.make_async_copy(source, place, out_sem.at[i, receiver, 2 * p + half])
                )
                low += count
            return copies

        sends.append(send)
        for receiver in range(8):
            for half in range(2):
                segment = facts[1 + receiver * 8 + low + 4 * half]

                @pl.when(segment >= 0)
                def _():
                    for copy in send(receiver, half, pl.multiple_of(segment * 128, 128)):
                        copy.start()

    for i, shift in enumerate(shifts):
        low = (z + shift + 8) & 3
        for receiver in range(8):
            for half in range(2):

                @pl.when(facts[1 + receiver * 8 + low + 4 * half] >= 0)
                def _():
                    for copy in sends[i](receiver, half, 0):
                        copy.wait()


def fold(shifts, facts, maps, tiles, pieces, before, weight):
    rows, length = tiles[0].shape
    count = len(shifts)
    whole = pltpu.VMEM((count, rows, length), jnp.bfloat16)
    return pl.pallas_call(
        functools.partial(fold_body, shifts, pieces),
        in_specs=[pl.BlockSpec(memory_space=pltpu.SMEM), pl.BlockSpec(memory_space=pltpu.VMEM)]
        + [pl.BlockSpec(memory_space=pl.ANY)] * (len(tiles) + len(before)),
        out_specs=[pl.BlockSpec(memory_space=pl.ANY)] * len(pieces)
        + [pl.BlockSpec(memory_space=pltpu.SMEM)],
        out_shape=[pltpu.HBM((8, 8, piece, 128), jnp.bfloat16) for piece in pieces]
        + [jax.ShapeDtypeStruct((1,), jnp.int32)],
        scratch_shapes=[
            whole,
            whole,
            whole,
            pltpu.SemaphoreType.DMA((count,)),
            pltpu.SemaphoreType.DMA((count, 2)),
            pltpu.SemaphoreType.DMA((count, 8, 2 * len(pieces))),
        ],
        compiler_params=pltpu.CompilerParams(vmem_limit_bytes=VMEM),
        cost_estimate=pl.CostEstimate(
            flops=weight * 2 * count * rows * length * length,
            bytes_accessed=count * rows * (4 * length + 16 * 256),
            transcendentals=0,
        ),
        input_output_aliases={2 + len(tiles) + p: p for p in range(len(before))},
        name="fold",
    )(facts, maps, *tiles, *before)


def nothing(*refs):
    pass


def joined(block, others, kind=jax.ShapeDtypeStruct):
    held = pl.BlockSpec(memory_space=pl.ANY)
    return pl.pallas_call(
        nothing,
        in_specs=[held] * (1 + len(others)),
        out_specs=held,
        out_shape=kind(block.shape, block.dtype),
        input_output_aliases={0: 0},
        compiler_params=pltpu.CompilerParams(vmem_limit_bytes=VMEM),
        name="joined",
    )(block, *others)


def halves_body(first, second, _, first_out, second_out, sem):
    cut = first_out.shape[0]
    copies = (
        pltpu.make_async_copy(first.at[pl.ds(0, cut)], first_out, sem.at[0]),
        pltpu.make_async_copy(second.at[pl.ds(cut, cut)], second_out, sem.at[1]),
    )
    for copy in copies:
        copy.start()
    for copy in copies:
        copy.wait()


def halves(first, second, after):
    rows, length = first.shape
    held = pl.BlockSpec(memory_space=pl.ANY)
    part = jax.ShapeDtypeStruct((rows // 2, length), first.dtype)
    return pl.pallas_call(
        halves_body,
        in_specs=[held] * 3,
        out_specs=[held] * 2,
        out_shape=[part] * 2,
        scratch_shapes=[pltpu.SemaphoreType.DMA((2,))],
        compiler_params=pltpu.CompilerParams(vmem_limit_bytes=VMEM),
        name="halves",
    )(first, second, after)


def ladder_body(facts, maps, blocks, received, ladder, sent, operand, rounded, held, sem, held_sem):
    length = rounded.shape[1]
    parts = held_sem.shape[0]
    depth = held.shape[0] // parts

    def place(k):
        tile = facts[65 + k]
        z, ket = tile >> 3, tile & 7
        slot = 2 * ((z - facts[0] + 8) & 3) + (z >> 2)
        where = operand.at[:, pl.ds(k * 128, 128)]
        return pltpu.make_async_copy(received.at[ket, slot], where, sem.at[k])

    def bring(i):
        rows = pl.ds(i * depth, depth)
        return pltpu.make_async_copy(blocks.at[rows], held.at[rows], held_sem.at[i])

    each = depth // 128
    for i in range(parts):
        for k in range(i * each, (i + 1) * each):
            place(k).start()
        bring(i).start()
    for i in range(parts):
        for k in range(i * each, (i + 1) * each):
            place(k).wait()
        bring(i).wait()
        rows = slice(i * depth, (i + 1) * depth)
        for low in range(0, length, COLS):
            columns = slice(low, low + COLS)
            total = jnp.dot(operand[:, rows], held[rows, columns], preferred_element_type=jnp.float32)
            if i:
                total += ladder[:, columns]
            ladder[:, columns] = total
            if i == parts - 1:
                rounded[:, columns] = total.astype(jnp.bfloat16)
    for low in range(0, length, COLS):
        columns = slice(low, low + COLS)
        picks = one_hot(maps[4, :, columns], length, COLS)
        moved = jnp.dot(rounded[...], picks, preferred_element_type=jnp.float32)
        sent[:, columns] = moved.astype(jnp.bfloat16)


def ladder_of(facts, maps, blocks, received):
    depth, length = blocks.shape
    rows = received.shape[2]
    vmem = pl.BlockSpec(memory_space=pltpu.VMEM)
    return pl.pallas_call(
        ladder_body,
        in_specs=[
            pl.BlockSpec(memory_space=pltpu.SMEM),
            vmem,
            pl.BlockSpec(memory_space=pl.ANY),
            pl.BlockSpec(memory_space=pl.ANY),
        ],
        out_specs=[vmem, vmem],
        out_shape=[
            pltpu.HBM((rows, length), jnp.float32),
            jax.ShapeDtypeStruct((rows, length), jnp.bfloat16),
        ],
        scratch_shapes=[
            pltpu.VMEM((rows, depth), jnp.bfloat16),
            pltpu.VMEM((rows, length), jnp.bfloat16),
            pltpu.VMEM((depth, length), jnp.bfloat16),
            pltpu.SemaphoreType.DMA((depth // 128,)),
            pltpu.SemaphoreType.DMA((4,)),
        ],
        compiler_params=pltpu.CompilerParams(vmem_limit_bytes=60 * 1024 * 1024),
        cost_estimate=pl.CostEstimate(
            flops=2 * rows * depth * length,
            bytes_accessed=2 * depth * (rows + length),
            transcendentals=0,
        ),
        name="ladder",
    )(facts, maps, blocks, received)


def update_body(low, *refs):
    own, ladder, partner, direction, occupied, virtual = refs[:6]
    out, fresh, sem = refs[-3:]
    rows = fresh.shape[0]
    step = 32
    copies = []
    for start in range(0, rows, step):
        block = slice(start, start + step)
        residual = ladder[block] + direction[0] * partner[block].astype(jnp.float32)
        denominator = occupied[block] - virtual[0:1, :] - virtual[1:2, :]
        new = own[block].astype(jnp.float32) + residual / denominator
        fresh[block] = new.astype(jnp.bfloat16)
        copies.append(
            pltpu.make_async_copy(
                fresh.at[pl.ds(start, step)], out.at[pl.ds(low + start, step)], sem.at[start // step]
            )
        )
        copies[-1].start()
    for copy in copies:
        copy.wait()


def update(low, total, own, ladder, partner, direction, occupied, virtual, before):
    rows, length = ladder.shape
    vmem, held = pl.BlockSpec(memory_space=pltpu.VMEM), pl.BlockSpec(memory_space=pl.ANY)
    return pl.pallas_call(
        functools.partial(update_body, low),
        in_specs=[vmem, vmem, vmem, pl.BlockSpec(memory_space=pltpu.SMEM), vmem, vmem]
        + [held] * len(before),
        out_specs=held,
        out_shape=pltpu.HBM((total, length), jnp.bfloat16),
        scratch_shapes=[pltpu.VMEM((rows, length), jnp.bfloat16), pltpu.SemaphoreType.DMA((rows // 32,))],
        input_output_aliases={6: 0} if before else {},
        compiler_params=pltpu.CompilerParams(vmem_limit_bytes=VMEM),
        cost_estimate=pl.CostEstimate(
            flops=8 * rows * length, bytes_accessed=10 * rows * length, transcendentals=0
        ),
        name="update",
    )(own, ladder, partner, direction, occupied, virtual, *before)


def shifted(block, by):
    return lax.ppermute(block, "bra", [(i, (i + by) % 8) for i in range(8)])


def energies(table, indices):
    number = lax.broadcasted_iota(jnp.int32, (table.shape[0], 1), 0)
    return jnp.sum(jnp.where(number == indices[None, :], table[:, None], 0.0), axis=0)


def local(
    amplitudes, integrals, screen_list, block_owner, mirror_map, pair_virt, vir_energy, pair_energy
):
    z, ket = lax.axis_index("bra"), lax.axis_index("ket")
    own = amplitudes[:, 0, :]
    rows, length = own.shape
    all_blocks = lax.all_gather(integrals[0], "pair", axis=0, tiled=True).reshape(-1, length)

    wanted = lax.all_gather(block_owner[0] * 16 + screen_list[0], "ket", axis=0)
    served = jnp.arange(8, dtype=jnp.int32) * 8 + ket
    match = (wanted >> 4)[:, None, :] == served[None, :, None]
    asked = jnp.max(jnp.where(match, wanted[:, None, :] & 15, -1), axis=2)
    facts = jnp.concatenate([z.astype(jnp.int32)[None], asked.reshape(-1), block_owner[0]])
    grid_maps = mirror_map.reshape(2, 4, 8, length)
    half_maps = lax.dynamic_index_in_dim(grid_maps, z >> 2, 0, keepdims=False)
    maps = lax.dynamic_index_in_dim(half_maps, ket, 1, keepdims=True)
    send_map = lax.dynamic_index_in_dim(mirror_map, ((z + 4) & 7) * 8 + ket, 0, keepdims=True)
    maps = jnp.concatenate([maps, send_map[None]])

    direction = jnp.where(z >= 4, 1.0, -1.0).astype(jnp.float32)
    first = energies(vir_energy, pair_virt[0, 0])
    second = energies(vir_energy, pair_virt[0, 1])
    virtual = jnp.stack([first, second])
    chunks = ((224,), (160,))
    steps, folds, low = [], [], 0
    for pieces in chunks:
        part = own[low : low + sum(pieces)]
        low += sum(pieces)
        if steps:
            part = joined(part, steps[-1][3], pltpu.HBM)
        one = (shifted(part, -1), shifted(part, 1))
        two = (shifted(one[0], -1), shifted(one[1], 1))
        weight = WEIGHT if steps else 1
        *slots, done = fold((2,), facts, maps, two, pieces, (), weight)
        three = (shifted(two[0], -1), shifted(two[1], 1))
        upper, lower = halves(*three, done)
        far = (shifted(upper, -1), shifted(lower, 1))
        odd = (one[0], three[1], three[0], one[1])
        *slots, _ = fold((1, 3), facts, maps, odd, pieces, slots, weight)
        steps.append((part, one, three, far))
        folds.append(slots)
    fresh, low, last = (), 0, ()
    for i, (part, one, three, far) in enumerate(steps):
        weight = WEIGHT if i else 1
        *slots, _ = fold((0,), facts, maps, (part, *far), chunks[i], folds[i], weight)
        for piece in slots:
            if last:
                piece = joined(piece, last, pltpu.HBM)
            received = lax.all_to_all(piece, "ket", split_axis=0, concat_axis=0, tiled=True)
            ladder, sent = ladder_of(facts, maps, all_blocks, received)
            last = (received,)
            partner = shifted(sent, 4)
            chunk = own[low : low + piece.shape[2]]
            occupied = pair_energy[low : low + piece.shape[2], None]
            new = update(
                low, rows, chunk, ladder, partner, direction[None], occupied, virtual, fresh
            )
            fresh = (new,)
            low += piece.shape[2]
    return new[:, None, :]


def solution(mesh):
    placed = (
        P("pair", ("bra", "ket"), None),
        P(("bra", "ket"), "pair", None, None),
        P(("bra", "ket"), None),
        P(("bra", "ket"), None),
        P(),
        P(("bra", "ket"), None, None),
        P(),
        P("pair"),
    )
    return jax.shard_map(
        local,
        mesh=mesh,
        in_specs=placed,
        out_specs=P("pair", ("bra", "ket"), None),
        check_vma=False,
    )
```
